128 devices in a mesh: gx: 16 (over z, x), gy: 8 (over y, core).
Axes of the slice: x: 4, y: 4, z: 4, core: 2. Of those that a mesh axis runs over, the one named last changes fastest.
Arguments:
- part_feat: bfloat16 [64, 1048576], P(None, ('gx', 'gy')), may hold values from -6 to 6
- target: bfloat16 [64, 1048576], P(None, ('gx', 'gy')), may hold values from -6 to 6
- block_tile: int32 [8192, 1], P(('gx', 'gy')), may hold values from 0 to 127; in each aligned block of 64 rows (0 to 63, 64 to 127, ...) at most 2 rows name the same one
- block_patch: int32 [8192], P(('gx', 'gy')), may hold values from 0 to 31
- cell_idx: int32 [8192, 128], P(('gx', 'gy')), may hold values from 0 to 127
- block_fill: int32 [8192], P(('gx', 'gy')), may hold values from 64 to 128
- conv_in: bfloat16 [9, 64, 64], replicated, may hold values from -0.25 to 0.25
- conv_mid: bfloat16 [9, 64, 64], replicated, may hold values from -0.25 to 0.25
- conv_out: bfloat16 [9, 64, 64], replicated, may hold values from -0.25 to 0.25
- mlp_grid: bfloat16 [64, 128], replicated, may hold values from -0.5 to 0.5
- mlp_part: bfloat16 [64, 128], replicated, may hold values from -0.5 to 0.5
- mlp_out: bfloat16 [128, 64], replicated, may hold values from -0.5 to 0.5
Outputs:
- pred: bfloat16 [64, 1048576], P(None, ('gx', 'gy'))
- grad_conv_in: float32 [9, 64, 64], replicated
- grad_conv_mid: float32 [9, 64, 64], replicated
- grad_conv_out: float32 [9, 64, 64], replicated
- grad_mlp_grid: float32 [64, 128], replicated
- grad_mlp_part: float32 [64, 128], replicated
- grad_mlp_out: float32 [128, 64], replicated
The draws below stay inside these ranges and needn't reach their ends.
Inputs may be any that keep to these rules, and one draw needn't show every extreme that they name: `block_tile`: among the 64 blocks of one device no tile is named by more than 2 blocks, a bound that some block reaches.
All inputs are finite; a program needn't handle non-finite values.
Results may differ from the reference program's by a relative error of at most 0.009.
Values may be sent and summed in bfloat16 or wider, within the bound.
No kernel may reach another device: no remote copies, remote signals or barrier semaphores. Data moves between devices by JAX's collectives and lax.ppermute only.
A program may use at most 128 MiB of HBM per device.

```python
import math
import jax
import jax.numpy as jnp
import numpy as np
from jax import lax

CH = 64
HID = 128
PR = 8
PC = 16
CR = 16
CC = 256
PB = 64
CAP = 2
PCELL = 128
NPATCH = 32
NBLK = 8192
NPART = 1048576
N_GX = 16
N_GY = 8
DEVICES = 128


def set_ends(array, rng, least, high):
    index_at = [jax.random.randint(jax.random.fold_in(rng, axis), (), 0, length) for axis, length in enumerate(array.shape)]
    longest = array.shape.index(max(array.shape))
    next_to = index_at[:longest] + [(index_at[longest] + 1) % array.shape[longest]] + index_at[longest + 1:]
    return array.at[tuple(index_at)].set(least).at[tuple(next_to)].set(high)


def block_scale(own_key, shape, cuts, low, largest):
    level, own = 1.0, jax.random.fold_in(own_key, 6)
    for axis_at, parts in cuts:
        draws = jnp.exp(jax.random.uniform(jax.random.fold_in(own, axis_at), (parts,), jnp.float32, low / len(cuts), largest / len(cuts)))
        level = level * jnp.repeat(draws, shape[axis_at] // parts).reshape([-1 if axis == axis_at else 1 for axis in range(len(shape))])
    return level


def routed_block(key, own, number, rows, amount, top, bound, lean):
    sequence = jax.random.permutation(key, amount)
    crowded, usual = shares(amount, rows * top, bound, lean, True), shares(amount, rows * top, bound, lean, False)
    places = jnp.arange(amount)

    def named(lengths, rotation):
        used = int((lengths > 0).sum())
        fixed = max(1, used // 4)
        moved = fixed + (places - fixed + rotation * (used - fixed)) % max(1, amount - fixed)
        return jnp.zeros((amount,), jnp.int32).at[sequence[jnp.where(places < fixed, places, moved)]].set(jnp.asarray(lengths, jnp.int32))

    lengths = jnp.where(number % 4 == 0, named(crowded, number // 4), named(usual, number - number // 4 - 1))
    mixed = jax.random.permutation(jax.random.fold_in(own, 3), amount)
    giver, receiver = mixed[0:amount // 2 * 2:2], mixed[1:amount // 2 * 2:2]
    room = jnp.minimum(lengths[giver] - 1, bound - lengths[receiver]) // 2
    room = jnp.where((giver == sequence[0]) | (receiver == sequence[0]) | (lengths[receiver] == 0), 0, jnp.maximum(room, 0))
    moved = jax.random.randint(jax.random.fold_in(own, 4), (amount // 2,), 0, 1 << 20) % (room + 1)
    lengths = lengths.at[giver].add(-moved).at[receiver].add(moved)
    members = jnp.searchsorted(jnp.cumsum(lengths), jnp.arange(rows * top), side="right").astype(jnp.int32)
    grid = members.reshape(top, rows).T
    grid = grid[jax.random.permutation(jax.random.fold_in(own, 1), rows)]
    rotation = jax.random.randint(jax.random.fold_in(own, 2), (rows, 1), 0, top)
    return jnp.take_along_axis(grid, (jnp.arange(top)[None, :] + rotation) % top, axis=1)


def shares(amount, total, bound, skew, full):
    portions = [(1 << 20) // math.isqrt(standing ** skew) + 1 for standing in range(1, amount + 1)]
    largest = bound if full else min(bound, max(-(-total // amount), total * portions[0] // sum(portions)))
    least = 1 if total - largest >= amount - 1 else 0
    given, rest = [largest] + [least] * (amount - 1), total - largest - least * (amount - 1)
    while rest > 0:
        candidates = [i for i in range(1, amount) if given[i] < largest] or [i for i in range(1, amount) if given[i] < bound]
        mass, budget = sum([portions[i] for i in candidates]), rest
        for i in candidates:
            more = min(bound - given[i], max(1, budget * portions[i] // mass), rest)
            given[i] = given[i] + more
            rest = rest - more
    return np.array(given)


def noise(own_key, dims, deviation, limit, split=(), kind=jnp.bfloat16):
    entries = deviation * jax.random.normal(own_key, dims, jnp.float32)
    if split:
        entries = entries * block_scale(own_key, dims, split, -0.22, 0.18)
    return jnp.clip(entries, -limit, limit).astype(kind)


def setup_inputs(seed: int = 0) -> dict:
    seeds = jax.random.split(jax.random.key(seed), 13)
    part_feat = noise(seeds[0], (CH, NPART), 1.0, 6.0, ((1, 128),))
    target = noise(seeds[1], (CH, NPART), 1.0, 6.0, ((1, 128),))
    block_tile_keys = jax.random.split(jax.random.fold_in(seeds[2], 1), NBLK // PB)
    block_tile_turns = jax.random.permutation(jax.random.fold_in(seeds[2], 3), NBLK // PB)
    block_tile = jax.vmap(lambda own, number: routed_block(jax.random.fold_in(seeds[2], 2), own, number, PB, DEVICES, 1, CAP, 2))(block_tile_keys, block_tile_turns).reshape((NBLK, 1))
    block_patch = set_ends(jax.random.randint(seeds[3], (NBLK,), 0, NPATCH), jax.random.fold_in(seeds[3], 1), 0, NPATCH - 1).astype(jnp.int32)
    cell_idx = set_ends(jax.random.randint(seeds[4], (NBLK, 128), 0, PCELL), jax.random.fold_in(seeds[4], 1), 0, PCELL - 1).astype(jnp.int32)
    block_fill = set_ends(jax.random.randint(seeds[5], (NBLK,), 64, 129), jax.random.fold_in(seeds[5], 1), 64, 128).astype(jnp.int32)
    conv_in = noise(seeds[6], (9, CH, CH), (9 * CH) ** -0.5, 0.25)
    conv_mid = noise(seeds[7], (9, CH, CH), (9 * CH) ** -0.5, 0.25)
    conv_out = noise(seeds[8], (9, CH, CH), (9 * CH) ** -0.5, 0.25)
    mlp_grid = noise(seeds[9], (CH, HID), (2 * CH) ** -0.5, 0.5)
    mlp_part = noise(seeds[10], (CH, HID), (2 * CH) ** -0.5, 0.5)
    mlp_out = noise(seeds[11], (HID, CH), HID ** -0.5, 0.5)
    return {"part_feat": part_feat, "target": target, "block_tile": block_tile, "block_patch": block_patch, "cell_idx": cell_idx, "block_fill": block_fill, "conv_in": conv_in, "conv_mid": conv_mid, "conv_out": conv_out, "mlp_grid": mlp_grid, "mlp_part": mlp_part, "mlp_out": mlp_out}


root_two_pi = 0.7978845608028654
cubic_coef = 0.044715

def gelu_value(value):
    return 0.5 * value * (1.0 + jnp.tanh(root_two_pi * (value + cubic_coef * value * value * value)))

def gelu_slope(value):
    inner = jnp.tanh(root_two_pi * (value + cubic_coef * value * value * value))
    return 0.5 * (1.0 + inner) + 0.5 * value * (1.0 - inner * inner) * root_two_pi * (1.0 + 3.0 * cubic_coef * value * value)

def product(form, left, right):
    return jnp.einsum(form, left.astype(jnp.float32), right.astype(jnp.float32), precision=lax.Precision.HIGHEST)

def conv_valid(padded, weight):
    kernel = weight.astype(jnp.float32).reshape(3, 3, weight.shape[1], weight.shape[2])
    result = lax.conv_general_dilated(padded.astype(jnp.float32)[None], kernel, (1, 1), 'VALID', dimension_numbers=('NCHW', 'HWIO', 'NCHW'), precision=lax.Precision.HIGHEST)
    return result[0]

def weight_term(padded, cotangent):
    result = lax.conv_general_dilated(padded.astype(jnp.float32)[None], cotangent.astype(jnp.float32)[None], (1, 1), 'VALID', dimension_numbers=('CNHW', 'IOHW', 'NCHW'), precision=lax.Precision.HIGHEST)
    return jnp.transpose(result, (2, 3, 0, 1)).reshape(9, result.shape[0], result.shape[1])

def flipped(weight):
    return jnp.transpose(weight[::-1], (0, 2, 1))

def pad_cells(field):
    return jnp.pad(field, ((0, 0), (1, 1), (1, 1)))

def pool_mean(field):
    return field.reshape(field.shape[0], field.shape[1] // 2, 2, field.shape[2] // 2, 2).mean(axis=(2, 4))

def pool_total(field):
    return field.reshape(field.shape[0], field.shape[1] // 2, 2, field.shape[2] // 2, 2).sum(axis=(2, 4))

def spread(field):
    return jnp.repeat(jnp.repeat(field, 2, axis=1), 2, axis=2)

def unet_forward(grid_input, conv_in, conv_mid, conv_out, border):
    input_pad = border(grid_input)
    first_pre = conv_valid(input_pad, conv_in)
    fine_act = gelu_value(first_pre).astype(jnp.bfloat16)
    coarse = pool_mean(fine_act.astype(jnp.float32)).astype(jnp.bfloat16)
    coarse_pad = border(coarse)
    mid_pre = conv_valid(coarse_pad, conv_mid)
    coarse_new = (coarse.astype(jnp.float32) + gelu_value(mid_pre)).astype(jnp.bfloat16)
    rebuilt = (fine_act.astype(jnp.float32) + spread(coarse_new.astype(jnp.float32) - coarse.astype(jnp.float32))).astype(jnp.bfloat16)
    rebuilt_pad = border(rebuilt)
    grid_output = conv_valid(rebuilt_pad, conv_out).astype(jnp.bfloat16)
    return (grid_output, (input_pad, first_pre, coarse_pad, mid_pre, rebuilt_pad))

def unet_backward(output_grad, saved, conv_in, conv_mid, conv_out, border):
    input_pad, first_pre, coarse_pad, mid_pre, rebuilt_pad = saved
    grad_out = weight_term(rebuilt_pad, output_grad)
    rebuilt_grad = conv_valid(border(output_grad), flipped(conv_out)).astype(jnp.bfloat16)
    mid_grad = (pool_total(rebuilt_grad.astype(jnp.float32)) * gelu_slope(mid_pre)).astype(jnp.bfloat16)
    grad_mid = weight_term(coarse_pad, mid_grad)
    coarse_grad = conv_valid(border(mid_grad), flipped(conv_mid))
    first_grad = ((rebuilt_grad.astype(jnp.float32) + 0.25 * spread(coarse_grad)) * gelu_slope(first_pre)).astype(jnp.bfloat16)
    grad_in = weight_term(input_pad, first_grad)
    return (grad_in, grad_mid, grad_out)

def particle_head(gathered, part_feat, target, living, mlp_grid, mlp_part, mlp_out, scale):
    hidden_pre = product('ch,cp->hp', mlp_grid, gathered) + product('ch,cp->hp', mlp_part, part_feat)
    hidden = gelu_value(hidden_pre).astype(jnp.bfloat16)
    pred_full = product('hc,hp->cp', mlp_out, hidden)
    pred_grad = (living * (pred_full - target.astype(jnp.float32)) * scale).astype(jnp.bfloat16)
    grad_out = product('hp,cp->hc', hidden, pred_grad)
    hidden_grad = (product('hc,cp->hp', mlp_out, pred_grad) * gelu_slope(hidden_pre)).astype(jnp.bfloat16)
    grad_grid = product('cp,hp->ch', gathered, hidden_grad)
    grad_part = product('cp,hp->ch', part_feat, hidden_grad)
    gathered_grad = product('ch,hp->cp', mlp_grid, hidden_grad).astype(jnp.bfloat16)
    return (pred_full.astype(jnp.bfloat16), grad_grid, grad_part, grad_out, gathered_grad)

def reference(part_feat, target, block_tile, block_patch, cell_idx, block_fill, conv_in, conv_mid, conv_out, mlp_grid, mlp_part, mlp_out):
    channels = part_feat.shape[0]
    grid_rows = CR * N_GY
    grid_cols = CC * N_GX
    all_cells = grid_rows * grid_cols
    patch_across = CC // PC
    within = jnp.arange(128, dtype=jnp.int32)
    alive = within[None, :] < block_fill[:, None]
    owners = block_tile[:, 0]
    row_base = owners % N_GY * CR + block_patch // patch_across * PR
    col_base = owners // N_GY * CC + block_patch % patch_across * PC
    row_at = row_base[:, None] + cell_idx // PC
    col_at = col_base[:, None] + cell_idx % PC
    places = jnp.where(alive, row_at * grid_cols + col_at, all_cells).reshape(-1).astype(jnp.int32)
    deposit = jnp.zeros((channels, all_cells + 1), jnp.float32).at[:, places].add(part_feat.astype(jnp.float32))
    counts = jnp.zeros((all_cells + 1,), jnp.float32).at[places].add(1.0)
    grid_input = (deposit[:, :all_cells] / (1.0 + counts[:all_cells])).astype(jnp.bfloat16).reshape(channels, grid_rows, grid_cols)
    grid_output, saved = unet_forward(grid_input, conv_in, conv_mid, conv_out, pad_cells)
    extended = jnp.concatenate([grid_output.reshape(channels, all_cells), jnp.zeros((channels, 1), jnp.bfloat16)], axis=1)
    gathered = extended[:, places]
    living = alive.reshape(1, -1).astype(jnp.float32)
    scale = 1.0 / jnp.sqrt(jnp.float32(part_feat.shape[1]))
    pred, grad_grid, grad_part, grad_out, gathered_grad = particle_head(gathered, part_feat, target, living, mlp_grid, mlp_part, mlp_out, scale)
    output_grad = jnp.zeros((channels, all_cells + 1), jnp.float32).at[:, places].add(gathered_grad.astype(jnp.float32))
    output_grad = output_grad[:, :all_cells].astype(jnp.bfloat16).reshape(channels, grid_rows, grid_cols)
    grad_in, grad_mid, grad_conv = unet_backward(output_grad, saved, conv_in, conv_mid, conv_out, pad_cells)
    return (pred, grad_in, grad_mid, grad_conv, grad_grid, grad_part, grad_out)
```

```python
import functools
import math

import jax
import jax.numpy as jnp
from jax import lax
from jax.experimental import pallas as pl
from jax.experimental.pallas import tpu as pltpu
from jax.sharding import PartitionSpec as P

CH = 64
HID = 128
CR = 16
CC = 256
LANES = 128
WIDE = 384
NPATCH = 32
META = 16
SLOT_ROWS = 2 * CH + META
HALO_IN = 5
HALO_OUT = 3
REDUCE_ROWS = 2048

root_two_pi = 0.7978845608028654
cubic_coef = 0.044715

VMEM_LIMIT = 56 * 1024 * 1024
BF = jnp.bfloat16
F32 = jnp.float32


def params():
    return pltpu.CompilerParams(vmem_limit_bytes=VMEM_LIMIT)


def cost(flops, moved, tanhs=0):
    return pl.CostEstimate(flops=flops, bytes_accessed=moved, transcendentals=tanhs)


def smem():
    return pl.BlockSpec(memory_space=pltpu.SMEM)


def vmem():
    return pl.BlockSpec(memory_space=pltpu.VMEM)


def whole(shape):
    return pl.BlockSpec(shape, lambda i: (0,) * len(shape))


def nt_dot(left, right):
    return lax.dot_general(left, right, (((1,), (1,)), ((), ())), preferred_element_type=F32)


def dot(left, right):
    return jnp.dot(left, right, preferred_element_type=F32)


def gelu_both(value):
    square = value * value
    inner = jnp.tanh(value * (root_two_pi + (root_two_pi * cubic_coef) * square))
    half = 0.5 + 0.5 * inner
    result = value * half
    bend = 2.0 * root_two_pi + (6.0 * cubic_coef * root_two_pi) * square
    return result, half + (result - result * half) * bend


def gelu_value(value):
    inner = jnp.tanh(value * (root_two_pi + (root_two_pi * cubic_coef) * (value * value)))
    return value * (0.5 + 0.5 * inner)


def lane_index(shape):
    return lax.broadcasted_iota(jnp.int32, shape, len(shape) - 1)


def place_blocks(tile_s, slot_s, count_s, blocks, devices):
    def clear(i, carry):
        count_s[i] = 0
        slot_s[2 * i] = -1
        slot_s[2 * i + 1] = -1
        return carry

    def place(b, carry):
        owner = tile_s[b]
        rank = count_s[owner]
        slot_s[2 * owner + rank] = b
        count_s[owner] = rank + 1
        return carry

    lax.fori_loop(0, devices, clear, 0, unroll=16)
    lax.fori_loop(0, blocks, place, 0, unroll=8)


def block_lanes(b):
    return pl.ds(pl.multiple_of(b * LANES, LANES), LANES)


def dispatch_kernel(blocks, devices, per, tile_s, patch_s, fill_s, cell_ref, feat_ref, out_ref, slot_s, count_s):
    step = pl.program_id(0)

    @pl.when(step == 0)
    def _():
        place_blocks(tile_s, slot_s, count_s, blocks, devices)

    def one(i, carry):
        owner = step * per + i
        row = lax.broadcasted_iota(jnp.int32, (META, LANES), 0)
        lane = lane_index((1, LANES))
        meta = jnp.zeros((META, LANES), F32)
        for r in range(2):
            b = slot_s[2 * owner + r]
            at = jnp.maximum(b, 0)
            out_ref[i, r * CH : (r + 1) * CH, :] = feat_ref[:, block_lanes(at)]
            fill = jnp.where(b >= 0, fill_s[at], 0)
            code = jnp.where(lane < fill, cell_ref[pl.ds(at, 1), :], -1).astype(F32)
            meta = jnp.where(row == r, code, meta)
            meta = jnp.where(row == 2 + r, patch_s[at].astype(F32), meta)
        out_ref[i, 2 * CH :, :] = meta.astype(BF)
        return carry

    lax.fori_loop(0, per, one, 0, unroll=16)


def route_scratch(devices):
    return [pltpu.SMEM((2 * devices,), jnp.int32), pltpu.SMEM((devices,), jnp.int32)]


def dispatch(tile, patch, fill, cells, features, devices):
    blocks = tile.shape[0]
    steps = 4
    per = devices // steps
    return pl.pallas_call(
        functools.partial(dispatch_kernel, blocks, devices, per),
        grid=(steps,),
        in_specs=[smem(), smem(), smem(), whole(cells.shape), whole(features.shape)],
        out_specs=pl.BlockSpec((per, SLOT_ROWS, LANES), lambda i: (i, 0, 0)),
        out_shape=jax.ShapeDtypeStruct((devices, SLOT_ROWS, LANES), BF),
        scratch_shapes=route_scratch(devices),
        compiler_params=params(),
        cost_estimate=cost(0, 6 << 20),
        name="dispatch",
    )(tile, patch, fill, cells, features)


def dispatch_target_kernel(blocks, devices, per, tile_s, feat_ref, first_ref, second_ref, slot_s, count_s):
    step = pl.program_id(0)

    @pl.when(step == 0)
    def _():
        place_blocks(tile_s, slot_s, count_s, blocks, devices)

    def one(i, carry):
        owner = step * per + i
        for r, out_ref in enumerate((first_ref, second_ref)):
            at = jnp.maximum(slot_s[2 * owner + r], 0)
            out_ref[i] = feat_ref[:, block_lanes(at)]
        return carry

    lax.fori_loop(0, per, one, 0, unroll=16)


def dispatch_target(tile, features, devices):
    blocks = tile.shape[0]
    steps = 4
    per = devices // steps
    shape = jax.ShapeDtypeStruct((devices, CH, LANES), BF)
    spec = pl.BlockSpec((per, CH, LANES), lambda i: (i, 0, 0))
    return pl.pallas_call(
        functools.partial(dispatch_target_kernel, blocks, devices, per),
        grid=(steps,),
        in_specs=[smem(), whole(features.shape)],
        out_specs=[spec, spec],
        out_shape=[shape, shape],
        scratch_shapes=route_scratch(devices),
        compiler_params=params(),
        cost_estimate=cost(0, 6 << 20),
        name="dispatch_target",
    )(tile, features)


def home_kernel(blocks, devices, tile_s, got_ref, feat_ref, w_hidden, w_pred, out_ref, pair, count_s):
    def clear(i, carry):
        count_s[i] = 0
        return carry

    lax.fori_loop(0, devices, clear, 0, unroll=16)

    def one(b, carry):
        owner = tile_s[b]
        rank = count_s[owner]
        count_s[owner] = rank + 1
        rows = pl.ds(pl.multiple_of(rank * CH, CH), CH)
        pair[:CH, block_lanes(b)] = got_ref[owner, rows, :]
        return carry

    lax.fori_loop(0, blocks, one, 0, unroll=8)
    pair[CH:, :] = feat_ref[...]
    span = 2048
    for start in range(0, blocks * LANES, span):
        lanes = slice(start, start + span)
        value = gelu_value(dot(w_hidden[...], pair[:, lanes])).astype(BF)
        out_ref[:, lanes] = dot(w_pred[...], value).astype(BF)


def home_predictions(tile, got, features, w_hidden, w_pred, devices):
    blocks = tile.shape[0]
    return pl.pallas_call(
        functools.partial(home_kernel, blocks, devices),
        in_specs=[smem()] + [vmem()] * 4,
        out_specs=vmem(),
        out_shape=jax.ShapeDtypeStruct((CH, blocks * LANES), BF),
        scratch_shapes=[
            pltpu.VMEM((2 * CH, blocks * LANES), BF),
            pltpu.SMEM((devices,), jnp.int32),
        ],
        compiler_params=params(),
        cost_estimate=cost(2 * 8192 * 128 * 192, 8 << 20, 8192 * 128),
        name="home_predictions",
    )(tile, got, features, w_hidden, w_pred)


def prepare_kernel(conv_in, conv_mid, conv_out, mlp_grid, mlp_part, mlp_out_t, w_in, w_mid, w_out, f_mid, f_out, w_hidden, w_back):
    for conv, out, flip in ((conv_in, w_in, None), (conv_mid, w_mid, f_mid), (conv_out, w_out, f_out)):
        for dr in range(3):
            for dq in range(3):
                rows = slice(dq * CH, (dq + 1) * CH)
                lanes = slice(dr * CH, (dr + 1) * CH)
                out[rows, lanes] = conv[3 * dr + dq].astype(F32).T.astype(BF)
                if flip is not None:
                    flip[rows, lanes] = conv[8 - 3 * dr - dq]
    w_hidden[:, :CH] = mlp_grid[...].astype(F32).T.astype(BF)
    w_hidden[:, CH:] = mlp_part[...].astype(F32).T.astype(BF)
    w_back[...] = mlp_out_t[...].astype(F32).T.astype(BF)


def prepare(*weights):
    square = jax.ShapeDtypeStruct((3 * CH, 3 * CH), BF)
    shapes = [square] * 5 + [
        jax.ShapeDtypeStruct((HID, 2 * CH), BF),
        jax.ShapeDtypeStruct((HID, CH), BF),
    ]
    return pl.pallas_call(
        prepare_kernel,
        in_specs=[vmem()] * len(weights),
        out_specs=[vmem()] * len(shapes),
        out_shape=shapes,
        compiler_params=params(),
        cost_estimate=cost(0, 1 << 20),
        name="prepare",
    )(*weights)


def swap_blocks(parts):
    parts = list(parts)
    group = lane_index(parts[0].shape) // 16
    for s in (4, 2, 1):
        keep = (group & s) == 0
        for i in range(8):
            if i & s:
                continue
            a, b = parts[i], parts[i + s]
            parts[i] = jnp.where(keep, a, pltpu.roll(b, s * 16, 1))
            parts[i + s] = jnp.where(keep, pltpu.roll(a, LANES - s * 16, 1), b)
    return parts


def patches_to_rows(patch_of, own_ref):
    for part in range(4):
        first, half = part // 2, part % 2
        rows = swap_blocks([patch_of(first * 16 + half * 8 + k) for k in range(8)])
        for r in range(8):
            own_ref[first * 8 + r, :, half * LANES : (half + 1) * LANES] = rows[r].astype(BF)


def write_strips(width, own_ref, head_ref, tail_ref, left_ref, right_ref):
    for r in range(width):
        for half in range(2):
            lanes = slice(half * LANES, (half + 1) * LANES)
            head_ref[2 * r + half] = own_ref[r, :, lanes]
            tail_ref[2 * r + half] = own_ref[CR - width + r, :, lanes]
    group = lane_index((CH, LANES)) // 8
    left = jnp.zeros((CH, LANES), F32)
    right = jnp.zeros((CH, LANES), F32)
    for r in range(CR):
        piece = own_ref[r, :, :LANES].astype(F32)
        left = jnp.where(group == r, pltpu.roll(piece, 8 * r, 1) if r else piece, left)
        piece = own_ref[r, :, LANES:].astype(F32)
        turn = (8 * r + 8) % LANES
        right = jnp.where(group == r, pltpu.roll(piece, turn, 1) if turn else piece, right)
    left_ref[0] = left.astype(BF)
    right_ref[0] = right.astype(BF)


def strip_shapes(width):
    return [
        jax.ShapeDtypeStruct((CR, CH, CC), BF),
        jax.ShapeDtypeStruct((2 * width, CH, LANES), BF),
        jax.ShapeDtypeStruct((2 * width, CH, LANES), BF),
        jax.ShapeDtypeStruct((1, CH, LANES), BF),
        jax.ShapeDtypeStruct((1, CH, LANES), BF),
    ]


def exchange(head, tail, left, right):
    def ahead(value, axis):
        count = lax.axis_size(axis)
        return lax.ppermute(value, axis, [(i, i + 1) for i in range(count - 1)])

    def behind(value, axis):
        count = lax.axis_size(axis)
        return lax.ppermute(value, axis, [(i + 1, i) for i in range(count - 1)])

    from_left = ahead(right, "gx")
    from_right = behind(left, "gx")
    above = ahead(tail, "gy")
    below = behind(head, "gy")
    sides = jnp.concatenate([from_left, from_right], axis=0)
    return above, below, sides, ahead(sides, "gy"), behind(sides, "gy")


def side_lanes(left, right, r):
    lane = lane_index((CH, LANES))
    turn_right = (LANES - 8 * r) % LANES
    turn_left = (120 - 8 * r) % LANES
    right = pltpu.roll(right, turn_right, 1) if turn_right else right
    left = pltpu.roll(left, turn_left, 1) if turn_left else left
    return jnp.where(lane < 8, right, jnp.where(lane >= 120, left, 0.0)).astype(BF)


def fill_wide(width, wide, own_ref, above_ref, below_ref, sides_ref, above_sides, below_sides):
    left, right = sides_ref[0].astype(F32), sides_ref[1].astype(F32)
    for r in range(CR):
        wide[width + r, :, :CC] = own_ref[r]
        wide[width + r, :, CC:] = side_lanes(left, right, r)
    left, right = above_sides[0].astype(F32), above_sides[1].astype(F32)
    for r in range(width):
        wide[r, :, :LANES] = above_ref[2 * r]
        wide[r, :, LANES:CC] = above_ref[2 * r + 1]
        wide[r, :, CC:] = side_lanes(left, right, CR - width + r)
    left, right = below_sides[0].astype(F32), below_sides[1].astype(F32)
    for r in range(width):
        at = width + CR + r
        wide[at, :, :LANES] = below_ref[2 * r]
        wide[at, :, LANES:CC] = below_ref[2 * r + 1]
        wide[at, :, CC:] = side_lanes(left, right, r)


def conv_row(source, at, weight, shift):
    stacked = source[pl.ds(at, 3)].reshape(3 * CH, WIDE)
    terms = dot(weight, stacked)
    return (
        terms[CH : 2 * CH]
        + pltpu.roll(terms[:CH], shift, 1)
        + pltpu.roll(terms[2 * CH :], WIDE - shift, 1)
    )


def pair_sum(value):
    even = (lane_index(value.shape) & 1) == 0
    return value + jnp.where(even, pltpu.roll(value, WIDE - 1, 1), pltpu.roll(value, 1, 1))


def column_mask(gx, columns):
    lane = lane_index((1, WIDE))
    right = jnp.where(gx < columns - 1, 1.0, 0.0)
    left = jnp.where(gx > 0, 1.0, 0.0)
    return jnp.where(lane < CC, 1.0, jnp.where(lane < CC + 64, right, left))


def one_hot(code):
    cell = lax.broadcasted_iota(jnp.int32, (LANES, LANES), 0).astype(F32).astype(BF)
    code = jnp.broadcast_to(code, (16, LANES)).astype(BF)
    match = cell.reshape(8, 16, LANES) == code[None]
    return jnp.where(match, jnp.ones((), BF), jnp.zeros((), BF)).reshape(LANES, LANES)


def deposit_kernel(per, last, got_ref, own, head, tail, left, right, patch_s, total):
    step = pl.program_id(0)

    @pl.when(step == 0)
    def _():
        total[...] = jnp.zeros_like(total)

    ones = jnp.ones((META, LANES), BF)

    def one(i, carry):
        meta = got_ref[i, 2 * CH :, :].astype(F32)
        for r in range(2):
            feat = jnp.concatenate([got_ref[i, r * CH : (r + 1) * CH, :], ones], axis=0)
            at = meta[2 + r, 0].astype(jnp.int32)
            patch_s[2 * (step * per + i) + r] = at
            total[at] += nt_dot(feat, one_hot(meta[r : r + 1]))
        return carry

    lax.fori_loop(0, per, one, 0, unroll=32)

    @pl.when(step == last)
    def _():
        def patch_of(a):
            value = total[a]
            return value[:CH] / (1.0 + value[CH : CH + 1])

        patches_to_rows(patch_of, own)
        write_strips(HALO_IN, own, head, tail, left, right)


SELF_PATCH = 1


def deposit(got):
    devices = got.shape[0]
    steps = 4
    per = devices // steps
    shapes = strip_shapes(HALO_IN)
    return pl.pallas_call(
        functools.partial(deposit_kernel, per, steps - 1),
        grid=(steps,),
        in_specs=[pl.BlockSpec((per, SLOT_ROWS, LANES), lambda i: (i, 0, 0))],
        out_specs=[whole(s.shape) for s in shapes] + [smem()],
        out_shape=shapes + [jax.ShapeDtypeStruct((2 * devices,), jnp.int32)],
        scratch_shapes=[pltpu.VMEM((NPATCH, CH + META, LANES), F32)],
        compiler_params=params(),
        cost_estimate=cost(2 * 256 * 80 * 128 * 128, 6 << 20),
        name="deposit",
    )(got)


def forward_kernel(
    columns,
    rows,
    where_s,
    own,
    above,
    below,
    sides,
    above_sides,
    below_sides,
    w_in,
    w_mid,
    w_out,
    patches,
    wide,
    coarse,
    rebuilt,
    slope_in,
    slope_mid,
    fine,
    grid_out,
):
    gx, gy = where_s[0], where_s[1]
    across = column_mask(gx, columns)
    fill_wide(HALO_IN, wide, own, above, below, sides, above_sides, below_sides)

    def row_mask(row):
        at = gy * CR + row
        return jnp.where(jnp.logical_and(at >= 0, at < rows * CR), across, 0.0)

    def first(g, carry):
        total = None
        for j in range(2):
            pre = conv_row(wide, 2 * g + j, w_in[...], 1)
            value, slope = gelu_both(pre)
            value = (value * row_mask(2 * g + j - 4)).astype(BF)
            fine[2 * g + j] = value
            slope_in[2 * g + j] = slope[:, :CC]
            value = value.astype(F32)
            total = value if j == 0 else total + value
        coarse[g] = (0.25 * pair_sum(total)).astype(BF)
        return carry

    lax.fori_loop(0, 12, first, 0, unroll=2)

    def middle(g, carry):
        pre = conv_row(coarse, g, w_mid[...], 2)
        value, slope = gelu_both(pre)
        slope_mid[g] = slope
        before = coarse[g + 1].astype(F32)
        change = (before + value).astype(BF).astype(F32) - before
        for j in range(2):
            row = fine[2 * g + 2 + j].astype(F32) + change
            rebuilt[2 * g + j] = (row * row_mask(2 * g + j - 2)).astype(BF)
        return carry

    lax.fori_loop(0, 10, middle, 0, unroll=2)

    def last(r, carry):
        grid_out[r] = conv_row(rebuilt, r + 1, w_out[...], 1)[:, :CC]
        return carry

    lax.fori_loop(0, CR, last, 0, unroll=4)
    for part in range(4):
        first_row, half = part // 2, part % 2
        lanes = slice(half * LANES, (half + 1) * LANES)
        found = swap_blocks([grid_out[first_row * 8 + r, :, lanes] for r in range(8)])
        for k in range(8):
            patches[first_row * 16 + half * 8 + k] = found[k].astype(BF)


def unet_forward(where, halo, w_in, w_mid, w_out, columns, rows):
    shapes = [
        jax.ShapeDtypeStruct((NPATCH, CH, LANES), BF),
        jax.ShapeDtypeStruct((CR + 2 * HALO_IN, CH, WIDE), BF),
        jax.ShapeDtypeStruct((12, CH, WIDE), BF),
        jax.ShapeDtypeStruct((20, CH, WIDE), BF),
        jax.ShapeDtypeStruct((24, CH, CC), F32),
        jax.ShapeDtypeStruct((10, CH, WIDE), F32),
    ]
    ins = (where, *halo, w_in, w_mid, w_out)
    return pl.pallas_call(
        functools.partial(forward_kernel, columns, rows),
        in_specs=[smem()] + [vmem()] * (len(ins) - 1),
        out_specs=[vmem()] * len(shapes),
        out_shape=shapes,
        scratch_shapes=[pltpu.VMEM((24, CH, WIDE), BF), pltpu.VMEM((CR, CH, CC), F32)],
        compiler_params=params(),
        cost_estimate=cost(2 * 50 * 192 * 192 * 384, 10 << 20, 34 * CH * WIDE),
        name="unet_forward",
    )(*ins)


def gather_kernel(per, patch_s, meta_ref, patches, out_ref):
    step = pl.program_id(0)

    def one(i, carry):
        meta = meta_ref[i].astype(F32)
        for r in range(2):
            patch = patch_s[2 * (step * per + i) + r]
            values = dot(patches[patch], one_hot(meta[r : r + 1]))
            out_ref[i, r * CH : (r + 1) * CH, :] = values.astype(BF)
        return carry

    lax.fori_loop(0, per, one, 0, unroll=32)


def gather(patch_at, got, patches):
    devices = got.shape[0]
    steps = 4
    per = devices // steps
    return pl.pallas_call(
        functools.partial(gather_kernel, per),
        grid=(steps,),
        in_specs=[
            smem(),
            pl.BlockSpec((per, META, LANES), lambda i: (i, 2 * CH // META, 0)),
            whole(patches.shape),
        ],
        out_specs=pl.BlockSpec((per, 2 * CH, LANES), lambda i: (i, 0, 0)),
        out_shape=jax.ShapeDtypeStruct((devices, 2 * CH, LANES), BF),
        compiler_params=params(),
        cost_estimate=cost(2 * 256 * 64 * 128 * 128, 6 << 20),
        name="gather",
    )(patch_at, got, patches)


GROUP = 16
GROUP_LANES = 2 * GROUP * LANES
PIECES = 1


def particle_kernel(
    last,
    scale,
    patch_s,
    got_ref,
    value_ref,
    first_ref,
    second_ref,
    w_hidden,
    w_pred,
    w_back,
    w_grid,
    own,
    head,
    tail,
    left,
    right,
    grads,
    total,
    pair,
    errors,
):
    step = pl.program_id(0)

    @pl.when(step == 0)
    def _():
        total[...] = jnp.zeros_like(total)
        grads[...] = jnp.zeros_like(grads)

    count = GROUP // PIECES
    span = 2 * count * LANES
    grad_hidden = jnp.zeros((HID, HID), F32)
    grad_pred = jnp.zeros((CH, HID), F32)
    for piece in range(PIECES):
        whole_lanes = slice(piece * span, (piece + 1) * span)
        codes = []
        for k in range(count):
            at = piece * count + k
            meta = got_ref[at, 2 * CH :, :].astype(F32)
            for r in range(2):
                rows = slice(r * CH, (r + 1) * CH)
                start = piece * span + (2 * k + r) * LANES
                lanes = slice(start, start + LANES)
                pair[:CH, lanes] = value_ref[at, rows, :]
                pair[CH:, lanes] = got_ref[at, rows, :]
                codes.append(meta[r : r + 1])
        inputs = pair[:, whole_lanes]
        hidden, slope = gelu_both(dot(w_hidden[...], inputs))
        hidden = hidden.astype(BF)
        pred = dot(w_pred[...], hidden)
        for k in range(count):
            for r, target_ref in enumerate((first_ref, second_ref)):
                slot = 2 * k + r
                lanes = slice(slot * LANES, (slot + 1) * LANES)
                live = jnp.where(codes[slot] >= 0.0, scale, 0.0)
                target = target_ref[piece * count + k].astype(F32)
                start = piece * span + slot * LANES
                errors[:, start : start + LANES] = (live * (pred[:, lanes] - target)).astype(BF)
        wrong = errors[:, whole_lanes]
        back = (dot(w_back[...], wrong) * slope).astype(BF)
        grad_hidden += nt_dot(inputs, back)
        grad_pred += nt_dot(wrong, hidden)
        given = dot(w_grid[...], back).astype(BF)
        for k in range(count):
            for r in range(2):
                slot = 2 * k + r
                patch = patch_s[2 * (step * GROUP + piece * count + k) + r]
                part = given[:, slot * LANES : (slot + 1) * LANES]
                total[patch] += nt_dot(part, one_hot(codes[slot]))
    grads[:HID] += grad_hidden
    grads[HID:] += grad_pred

    @pl.when(step == last)
    def _():
        patches_to_rows(lambda a: total[a], own)
        write_strips(HALO_OUT, own, head, tail, left, right)


def particles(patch_at, got, values, first, second, w_hidden, w_pred, w_back, w_grid, scale):
    devices = got.shape[0]
    steps = devices // GROUP
    half = pl.BlockSpec((GROUP, CH, LANES), lambda i: (i, 0, 0))
    shapes = strip_shapes(HALO_OUT) + [jax.ShapeDtypeStruct((HID + CH, HID), F32)]
    return pl.pallas_call(
        functools.partial(particle_kernel, steps - 1, scale),
        grid=(steps,),
        in_specs=[
            smem(),
            pl.BlockSpec((GROUP, SLOT_ROWS, LANES), lambda i: (i, 0, 0)),
            pl.BlockSpec((GROUP, 2 * CH, LANES), lambda i: (i, 0, 0)),
            half,
            half,
            whole(w_hidden.shape),
            whole(w_pred.shape),
            whole(w_back.shape),
            whole(w_grid.shape),
        ],
        out_specs=[whole(s.shape) for s in shapes],
        out_shape=shapes,
        scratch_shapes=[
            pltpu.VMEM((NPATCH, CH, LANES), F32),
            pltpu.VMEM((2 * CH, GROUP_LANES), BF),
            pltpu.VMEM((CH, GROUP_LANES), BF),
        ],
        compiler_params=params(),
        cost_estimate=cost(2 * 32768 * 128 * 700, 16 << 20, 32768 * 128),
        name="particles",
    )(patch_at, got, values, first, second, w_hidden, w_pred, w_back, w_grid)


def shifted(value, shift):
    value = jnp.concatenate([value, jnp.zeros((CH, LANES), F32)], axis=1)
    return jnp.concatenate(
        [pltpu.roll(value, WIDE - shift, 1), value, pltpu.roll(value, shift, 1)], axis=0
    ).astype(BF)


def out_terms_kernel(own, rebuilt, sum_out):
    sum_out[...] = jnp.zeros_like(sum_out)

    def one(r, carry):
        sum_out[:, : 3 * CH] += nt_dot(
            rebuilt[pl.ds(r + 1, 3)].reshape(3 * CH, WIDE), shifted(own[r].astype(F32), 1)
        )
        return carry

    lax.fori_loop(0, CR, one, 0, unroll=4)


def out_terms(own, rebuilt):
    return pl.pallas_call(
        out_terms_kernel,
        in_specs=[vmem(), vmem()],
        out_specs=vmem(),
        out_shape=jax.ShapeDtypeStruct((3 * CH, 2 * LANES), F32),
        compiler_params=params(),
        cost_estimate=cost(2 * 16 * 192 * 192 * 384, 10 << 20),
        name="out_terms",
    )(own, rebuilt)


def backward_kernel(
    columns,
    rows,
    where_s,
    own,
    above,
    below,
    sides,
    above_sides,
    below_sides,
    wide_in,
    coarse,
    slope_in,
    slope_mid,
    flip_mid,
    flip_out,
    particle_grads,
    sum_out,
    staged,
    wide,
    rebuilt_grad,
    mid_grad,
    first_grad,
    sum_in,
    sum_mid,
):
    gx, gy = where_s[0], where_s[1]
    across = column_mask(gx, columns)
    fill_wide(HALO_OUT, wide, own, above, below, sides, above_sides, below_sides)

    def pooled(g, carry):
        total = None
        for j in range(2):
            value = conv_row(wide, 2 * g + j, flip_out[...], 1).astype(BF)
            rebuilt_grad[2 * g + j] = value
            value = value.astype(F32)
            total = value if j == 0 else total + value
        at = gy * CR + 2 * g - 2
        mask = jnp.where(jnp.logical_and(at >= 0, at < rows * CR), across, 0.0)
        mid_grad[g] = (pair_sum(total) * slope_mid[g] * mask).astype(BF)
        return carry

    lax.fori_loop(0, 10, pooled, 0, unroll=2)

    def fine(g, carry):
        spread = 0.25 * conv_row(mid_grad, g, flip_mid[...], 2)[:, :CC]
        for j in range(2):
            value = rebuilt_grad[2 * g + 2 + j, :, :CC].astype(F32) + spread
            first_grad[2 * g + j] = (value * slope_in[2 * g + 4 + j]).astype(BF)
        return carry

    lax.fori_loop(0, 8, fine, 0, unroll=4)

    sum_in[...] = jnp.zeros_like(sum_in)
    sum_mid[...] = jnp.zeros_like(sum_mid)

    def fine_terms(r, carry):
        sum_in[:, : 3 * CH] += nt_dot(
            wide_in[pl.ds(r + HALO_IN - 1, 3)].reshape(3 * CH, WIDE),
            shifted(first_grad[r].astype(F32), 1),
        )
        return carry

    lax.fori_loop(0, CR, fine_terms, 0, unroll=4)
    even = (lane_index((CH, CC)) & 1) == 0

    def coarse_terms(g, carry):
        value = jnp.where(even, mid_grad[g + 1, :, :CC].astype(F32), 0.0)
        sum_mid[:, : 3 * CH] += nt_dot(
            coarse[pl.ds(g + 1, 3)].reshape(3 * CH, WIDE), shifted(value, 2)
        )
        return carry

    lax.fori_loop(0, 8, coarse_terms, 0, unroll=4)

    rows_each = 3 * CH
    for which, total in enumerate((sum_in, sum_mid, sum_out)):
        for half in range(2):
            start = (2 * which + half) * rows_each
            staged[start : start + rows_each] = total[
                :, half * LANES : (half + 1) * LANES
            ].astype(BF)
    start = 6 * rows_each
    staged[start : start + HID + CH] = particle_grads[...].astype(BF)
    staged[start + HID + CH :] = jnp.zeros((REDUCE_ROWS - start - HID - CH, LANES), BF)


def unet_backward(where, halo, saved, flip_mid, flip_out, particle_grads, sum_out, columns, rows):
    ins = (where, *halo, *saved, flip_mid, flip_out, particle_grads, sum_out)
    return pl.pallas_call(
        functools.partial(backward_kernel, columns, rows),
        in_specs=[smem()] + [vmem()] * (len(ins) - 1),
        out_specs=vmem(),
        out_shape=jax.ShapeDtypeStruct((REDUCE_ROWS, LANES), BF),
        scratch_shapes=[
            pltpu.VMEM((CR + 2 * HALO_OUT, CH, WIDE), BF),
            pltpu.VMEM((20, CH, WIDE), BF),
            pltpu.VMEM((10, CH, WIDE), BF),
            pltpu.VMEM((CR, CH, CC), BF),
            pltpu.VMEM((3 * CH, 2 * LANES), F32),
            pltpu.VMEM((3 * CH, 2 * LANES), F32),
        ],
        compiler_params=params(),
        cost_estimate=cost(2 * 70 * 192 * 192 * 384, 10 << 20),
        name="unet_backward",
    )(*ins)


def split_kernel(sums, grad_in, grad_mid, grad_out, grad_grid, grad_part, grad_pred):
    for which, out in enumerate((grad_in, grad_mid, grad_out)):
        for dr in range(3):
            start = 2 * which * 3 * CH + dr * CH
            low = sums[start : start + CH, :].astype(F32)
            out[3 * dr] = low[:, :CH]
            out[3 * dr + 1] = low[:, CH:]
            out[3 * dr + 2] = sums[start + 3 * CH : start + 4 * CH, :CH].astype(F32)
    start = 18 * CH
    grad_grid[...] = sums[start : start + CH, :].astype(F32)
    grad_part[...] = sums[start + CH : start + 2 * CH, :].astype(F32)
    grad_pred[...] = sums[start + 2 * CH : start + 3 * CH, :].astype(F32)


def split(sums):
    conv = jax.ShapeDtypeStruct((9, CH, CH), F32)
    mlp = jax.ShapeDtypeStruct((CH, HID), F32)
    shapes = [conv, conv, conv, mlp, mlp, mlp]
    return pl.pallas_call(
        split_kernel,
        in_specs=[vmem()],
        out_specs=[vmem()] * 6,
        out_shape=shapes,
        compiler_params=params(),
        cost_estimate=cost(0, 3 << 20),
        name="split",
    )(sums)


def swap(value):
    return lax.all_to_all(value, ("gx", "gy"), split_axis=0, concat_axis=0, tiled=True)


def shards(
    part_feat,
    target,
    block_tile,
    block_patch,
    cell_idx,
    block_fill,
    conv_in,
    conv_mid,
    conv_out,
    mlp_grid,
    mlp_part,
    mlp_out,
):
    nblocks = block_tile.shape[0]
    columns, rows = lax.axis_size("gx"), lax.axis_size("gy")
    devices = columns * rows
    tile = block_tile[:, 0]
    where = jnp.stack([lax.axis_index("gx"), lax.axis_index("gy")]).astype(jnp.int32)
    scale = 1.0 / math.sqrt(nblocks * LANES * devices)
    w_pred = mlp_out.T

    sent = dispatch(tile, block_patch, block_fill, cell_idx, part_feat, devices)
    sent_first, sent_second = dispatch_target(tile, target, devices)
    got = swap(sent)
    prepared = prepare(conv_in, conv_mid, conv_out, mlp_grid, mlp_part, w_pred)
    got, sent_first, sent_second, where, *prepared = lax.optimization_barrier(
        (got, sent_first, sent_second, where, *prepared)
    )
    w_in, w_mid, w_out, f_mid, f_out, w_hidden, w_back = prepared
    got_first = swap(sent_first)

    own, *strips, patch_at = deposit(got)
    halo = (own, *exchange(*strips))
    sent_second, *halo = lax.optimization_barrier((sent_second, *halo))
    got_second = swap(sent_second)
    patches, wide_in, coarse, rebuilt, slope_in, slope_mid = unet_forward(
        where, halo, w_in, w_mid, w_out, columns, rows
    )
    values = gather(patch_at, got, patches)
    got_values = swap(values)
    own, *strips, particle_grads = particles(
        patch_at, got, values, got_first, got_second, w_hidden, w_pred, w_back, mlp_grid, scale
    )
    halo = (own, *exchange(*strips))
    sum_out = out_terms(own, rebuilt)
    saved = (wide_in, coarse, slope_in, slope_mid)
    staged = unet_backward(
        where, halo, saved, f_mid, f_out, particle_grads, sum_out, columns, rows
    )
    staged, got_values = lax.optimization_barrier((staged, got_values))
    terms = swap(staged.reshape(devices, REDUCE_ROWS // devices, LANES))
    mine = jnp.sum(terms.astype(F32), axis=0).astype(BF)
    spread = swap(jnp.broadcast_to(mine[None], (devices, *mine.shape)))
    pred = home_predictions(tile, got_values, part_feat, w_hidden, w_pred, devices)
    *grads, grad_pred = split(spread.reshape(REDUCE_ROWS, LANES))
    return (pred, *grads, grad_pred.T)


def solution(mesh):
    return jax.shard_map(
        shards,
        mesh=mesh,
        in_specs=(
            P(None, ("gx", "gy")),
            P(None, ("gx", "gy")),
            P(("gx", "gy"), None),
            P(("gx", "gy")),
            P(("gx", "gy"), None),
            P(("gx", "gy")),
            P(),
            P(),
            P(),
            P(),
            P(),
            P(),
        ),
        out_specs=(P(None, ("gx", "gy")), P(), P(), P(), P(), P(), P()),
        check_vma=False,
    )
```

```python
import functools
import math

import jax
import jax.numpy as jnp
from jax import lax
from jax.experimental import pallas as pl
from jax.experimental.pallas import tpu as pltpu
from jax.sharding import PartitionSpec as P

CH = 64
HID = 128
CR = 16
CC = 256
LANES = 128
WIDE = 384
NPATCH = 32
META = 8
SLOT_ROWS = 2 * CH + META
HALO_IN = 5
HALO_OUT = 3
REDUCE_ROWS = 2048

root_two_pi = 0.7978845608028654
cubic_coef = 0.044715

VMEM_LIMIT = 56 * 1024 * 1024
BF = jnp.bfloat16
F32 = jnp.float32


def params():
    return pltpu.CompilerParams(vmem_limit_bytes=VMEM_LIMIT)


def cost(flops, moved, tanhs=0):
    return pl.CostEstimate(flops=flops, bytes_accessed=moved, transcendentals=tanhs)


def smem():
    return pl.BlockSpec(memory_space=pltpu.SMEM)


def vmem():
    return pl.BlockSpec(memory_space=pltpu.VMEM)


def whole(shape):
    return pl.BlockSpec(shape, lambda i: (0,) * len(shape))


def nt_dot(left, right):
    return lax.dot_general(left, right, (((1,), (1,)), ((), ())), preferred_element_type=F32)


def dot(left, right):
    return jnp.dot(left, right, preferred_element_type=F32)


def gelu_both(value):
    square = value * value
    inner = jnp.tanh(value * (root_two_pi + (root_two_pi * cubic_coef) * square))
    half = 0.5 + 0.5 * inner
    result = value * half
    bend = 2.0 * root_two_pi + (6.0 * cubic_coef * root_two_pi) * square
    return result, half + (result - result * half) * bend


def gelu_slope(half, result, square):
    bend = 2.0 * root_two_pi + (6.0 * cubic_coef * root_two_pi) * square
    return half + (result - result * half) * bend


def gelu_parts(value):
    square = value * value
    inner = jnp.tanh(value * (root_two_pi + (root_two_pi * cubic_coef) * square))
    half = 0.5 + 0.5 * inner
    return value * half, half, square


def gelu_value(value):
    inner = jnp.tanh(value * (root_two_pi + (root_two_pi * cubic_coef) * (value * value)))
    return value * (0.5 + 0.5 * inner)


def lane_index(shape):
    return lax.broadcasted_iota(jnp.int32, shape, len(shape) - 1)


def peer_of(tile, grid):
    columns, rows = grid
    return lax.rem(tile, rows) * columns + lax.div(tile, rows)


def place_blocks(tile_s, slot_s, count_s, blocks, grid):
    devices = grid[0] * grid[1]

    def clear(i, carry):
        count_s[i] = 0
        slot_s[2 * i] = -1
        slot_s[2 * i + 1] = -1
        return carry

    def place(b, carry):
        owner = peer_of(tile_s[b], grid)
        rank = count_s[owner]
        slot_s[2 * owner + rank] = b
        count_s[owner] = rank + 1
        return carry

    lax.fori_loop(0, devices, clear, 0, unroll=16)
    lax.fori_loop(0, blocks, place, 0, unroll=8)


def block_lanes(b):
    return pl.ds(pl.multiple_of(b * LANES, LANES), LANES)


def dispatch_kernel(blocks, grid, per, tile_s, patch_s, fill_s, cell_ref, feat_ref, out_ref, slot_s, count_s):
    step = pl.program_id(0)

    @pl.when(step == 0)
    def _():
        place_blocks(tile_s, slot_s, count_s, blocks, grid)

    def one(i, carry):
        owner = step * per + i
        row = lax.broadcasted_iota(jnp.int32, (META, LANES), 0)
        lane = lane_index((1, LANES))
        meta = jnp.zeros((META, LANES), F32)
        for r in range(2):
            b = slot_s[2 * owner + r]
            at = jnp.maximum(b, 0)
            out_ref[i, r * CH : (r + 1) * CH, :] = feat_ref[:, block_lanes(at)]
            fill = jnp.where(b >= 0, fill_s[at], 0)
            code = jnp.where(lane < fill, cell_ref[pl.ds(at, 1), :], -1).astype(F32)
            meta = jnp.where(row == r, code, meta)
            meta = jnp.where(row == 2 + r, patch_s[at].astype(F32), meta)
        out_ref[i, 2 * CH :, :] = meta.astype(BF)
        return carry

    lax.fori_loop(0, per, one, 0, unroll=16)


def route_scratch(devices):
    return [pltpu.SMEM((2 * devices,), jnp.int32), pltpu.SMEM((devices,), jnp.int32)]


def dispatch(tile, patch, fill, cells, features, grid):
    devices = grid[0] * grid[1]
    blocks = tile.shape[0]
    steps = 2
    per = devices // steps
    return pl.pallas_call(
        functools.partial(dispatch_kernel, blocks, grid, per),
        grid=(steps,),
        in_specs=[smem(), smem(), smem(), whole(cells.shape), whole(features.shape)],
        out_specs=pl.BlockSpec((per, SLOT_ROWS, LANES), lambda i: (i, 0, 0)),
        out_shape=jax.ShapeDtypeStruct((devices, SLOT_ROWS, LANES), BF),
        scratch_shapes=route_scratch(devices),
        compiler_params=params(),
        cost_estimate=cost(0, 6 << 20),
        name="dispatch",
    )(tile, patch, fill, cells, features)


def dispatch_target_kernel(blocks, grid, per, tile_s, feat_ref, out_ref, slot_s, count_s):
    step = pl.program_id(0)

    @pl.when(step == 0)
    def _():
        place_blocks(tile_s, slot_s, count_s, blocks, grid)

    def one(i, carry):
        owner = step * per + i
        for r in range(2):
            at = jnp.maximum(slot_s[2 * owner + r], 0)
            out_ref[i, r * CH : (r + 1) * CH, :] = feat_ref[:, block_lanes(at)]
        return carry

    lax.fori_loop(0, per, one, 0, unroll=16)


def dispatch_target(tile, features, grid):
    devices = grid[0] * grid[1]
    blocks = tile.shape[0]
    steps = 4
    per = devices // steps
    return pl.pallas_call(
        functools.partial(dispatch_target_kernel, blocks, grid, per),
        grid=(steps,),
        in_specs=[smem(), whole(features.shape)],
        out_specs=pl.BlockSpec((per, 2 * CH, LANES), lambda i: (i, 0, 0)),
        out_shape=jax.ShapeDtypeStruct((devices, 2 * CH, LANES), BF),
        scratch_shapes=route_scratch(devices),
        compiler_params=params(),
        cost_estimate=cost(0, 6 << 20),
        name="dispatch_target",
    )(tile, features)


def home_kernel(blocks, grid, tile_s, fill_s, cell_ref, got_ref, feat_ref, w_hidden, w_pred, out_ref, pair, count_s):
    def clear(i, carry):
        count_s[i] = 0
        return carry

    lax.fori_loop(0, grid[0] * grid[1], clear, 0, unroll=16)

    def one(b, carry):
        owner = peer_of(tile_s[b], grid)
        rank = count_s[owner]
        count_s[owner] = rank + 1
        rows = pl.ds(pl.multiple_of(rank * CH, CH), CH)
        code = jnp.where(lane_index((1, LANES)) < fill_s[b], cell_ref[pl.ds(b, 1), :], -1)
        values = dot(got_ref[owner, rows, :], one_hot(code.astype(F32)))
        pair[:CH, block_lanes(b)] = values.astype(BF)
        return carry

    lax.fori_loop(0, blocks, one, 0, unroll=16)
    pair[CH:, :] = feat_ref[...]
    span = 2048
    for start in range(0, blocks * LANES, span):
        lanes = slice(start, start + span)
        value = gelu_value(dot(w_hidden[...], pair[:, lanes])).astype(BF)
        out_ref[:, lanes] = dot(w_pred[...], value).astype(BF)


def home_predictions(tile, fill, cells, got, features, w_hidden, w_pred, grid):
    devices = grid[0] * grid[1]
    blocks = tile.shape[0]
    return pl.pallas_call(
        functools.partial(home_kernel, blocks, grid),
        in_specs=[smem(), smem()] + [vmem()] * 5,
        out_specs=vmem(),
        out_shape=jax.ShapeDtypeStruct((CH, blocks * LANES), BF),
        scratch_shapes=[
            pltpu.VMEM((2 * CH, blocks * LANES), BF),
            pltpu.SMEM((devices,), jnp.int32),
        ],
        compiler_params=params(),
        cost_estimate=cost(2 * 8192 * 128 * 192, 8 << 20, 8192 * 128),
        name="home_predictions",
    )(tile, fill, cells, got, features, w_hidden, w_pred)


def prepare_kernel(conv_in, conv_mid, conv_out, mlp_grid, mlp_part, mlp_out_t, w_in, w_mid, w_out, f_mid, f_out, w_hidden, w_back):
    for conv, out, flip in ((conv_in, w_in, None), (conv_mid, w_mid, f_mid), (conv_out, w_out, f_out)):
        for dr in range(3):
            for dq in range(3):
                rows = slice(dq * CH, (dq + 1) * CH)
                lanes = slice(dr * CH, (dr + 1) * CH)
                out[rows, lanes] = conv[3 * dr + dq].astype(F32).T.astype(BF)
                if flip is not None:
                    flip[rows, lanes] = conv[8 - 3 * dr - dq]
    w_hidden[:, :CH] = mlp_grid[...].astype(F32).T.astype(BF)
    w_hidden[:, CH:] = mlp_part[...].astype(F32).T.astype(BF)
    w_back[...] = mlp_out_t[...].astype(F32).T.astype(BF)


def prepare(*weights):
    square = jax.ShapeDtypeStruct((3 * CH, 3 * CH), BF)
    shapes = [square] * 5 + [
        jax.ShapeDtypeStruct((HID, 2 * CH), BF),
        jax.ShapeDtypeStruct((HID, CH), BF),
    ]
    return pl.pallas_call(
        prepare_kernel,
        in_specs=[vmem()] * len(weights),
        out_specs=[vmem()] * len(shapes),
        out_shape=shapes,
        compiler_params=params(),
        cost_estimate=cost(0, 1 << 20),
        name="prepare",
    )(*weights)


def swap_blocks(parts):
    parts = list(parts)
    group = lane_index(parts[0].shape) // 16
    for s in (4, 2, 1):
        keep = (group & s) == 0
        for i in range(8):
            if i & s:
                continue
            a, b = parts[i], parts[i + s]
            parts[i] = jnp.where(keep, a, pltpu.roll(b, s * 16, 1))
            parts[i + s] = jnp.where(keep, pltpu.roll(a, LANES - s * 16, 1), b)
    return parts


def patches_to_rows(patch_of, own_ref):
    for part in range(4):
        first, half = part // 2, part % 2
        rows = swap_blocks([patch_of(first * 16 + half * 8 + k) for k in range(8)])
        for r in range(8):
            own_ref[first * 8 + r, :, half * LANES : (half + 1) * LANES] = rows[r].astype(BF)


def write_strips(width, own_ref, head_ref, tail_ref, left_ref, right_ref):
    for r in range(width):
        for half in range(2):
            lanes = slice(half * LANES, (half + 1) * LANES)
            head_ref[2 * r + half] = own_ref[r, :, lanes]
            tail_ref[2 * r + half] = own_ref[CR - width + r, :, lanes]
    group = lane_index((CH, LANES)) // 8
    left = jnp.zeros((CH, LANES), F32)
    right = jnp.zeros((CH, LANES), F32)
    for r in range(CR):
        piece = own_ref[r, :, :LANES].astype(F32)
        left = jnp.where(group == r, pltpu.roll(piece, 8 * r, 1) if r else piece, left)
        piece = own_ref[r, :, LANES:].astype(F32)
        turn = (8 * r + 8) % LANES
        right = jnp.where(group == r, pltpu.roll(piece, turn, 1) if turn else piece, right)
    left_ref[0] = left.astype(BF)
    right_ref[0] = right.astype(BF)


def strip_shapes(width):
    return [
        jax.ShapeDtypeStruct((CR, CH, CC), BF),
        jax.ShapeDtypeStruct((2 * width, CH, LANES), BF),
        jax.ShapeDtypeStruct((2 * width, CH, LANES), BF),
        jax.ShapeDtypeStruct((1, CH, LANES), BF),
        jax.ShapeDtypeStruct((1, CH, LANES), BF),
    ]


def ahead(value, axis):
    count = lax.axis_size(axis)
    return lax.ppermute(value, axis, [(i, i + 1) for i in range(count - 1)])


def behind(value, axis):
    count = lax.axis_size(axis)
    return lax.ppermute(value, axis, [(i + 1, i) for i in range(count - 1)])


def exchange(head, tail, left, right, beside=None):
    from_left, from_right = ahead(right, "gx"), behind(left, "gx")
    above, below = ahead(tail, "gy"), behind(head, "gy")
    if beside is not None:
        from_left, from_right, beside = lax.optimization_barrier((from_left, from_right, beside))
    sides = jnp.concatenate([from_left, from_right], axis=0)
    return (above, below, sides, ahead(sides, "gy"), behind(sides, "gy")), beside


def side_lanes(left, right, r):
    lane = lane_index((CH, LANES))
    turn_right = (LANES - 8 * r) % LANES
    turn_left = (120 - 8 * r) % LANES
    right = pltpu.roll(right, turn_right, 1) if turn_right else right
    left = pltpu.roll(left, turn_left, 1) if turn_left else left
    return jnp.where(lane < 8, right, jnp.where(lane >= 120, left, 0.0)).astype(BF)


def fill_wide(width, wide, own_ref, above_ref, below_ref, sides, above_sides, below_sides):
    left, right = sides[0].astype(F32), sides[1].astype(F32)
    for r in range(CR):
        wide[width + r, :, :CC] = own_ref[r]
        wide[width + r, :, CC:] = side_lanes(left, right, r)
    left, right = above_sides[0].astype(F32), above_sides[1].astype(F32)
    for r in range(width):
        wide[r, :, :LANES] = above_ref[2 * r]
        wide[r, :, LANES:CC] = above_ref[2 * r + 1]
        wide[r, :, CC:] = side_lanes(left, right, CR - width + r)
    left, right = below_sides[0].astype(F32), below_sides[1].astype(F32)
    for r in range(width):
        at = width + CR + r
        wide[at, :, :LANES] = below_ref[2 * r]
        wide[at, :, LANES:CC] = below_ref[2 * r + 1]
        wide[at, :, CC:] = side_lanes(left, right, r)


def conv_row(source, at, weight, shift):
    stacked = source[pl.ds(at, 3)].reshape(3 * CH, WIDE)
    terms = dot(weight, stacked)
    return (
        terms[CH : 2 * CH]
        + pltpu.roll(terms[:CH], shift, 1)
        + pltpu.roll(terms[2 * CH :], WIDE - shift, 1)
    )


def pair_sum(value):
    even = (lane_index(value.shape) & 1) == 0
    return value + jnp.where(even, pltpu.roll(value, WIDE - 1, 1), pltpu.roll(value, 1, 1))


def column_mask(gx, columns):
    lane = lane_index((1, WIDE))
    right = jnp.where(gx < columns - 1, 1.0, 0.0)
    left = jnp.where(gx > 0, 1.0, 0.0)
    return jnp.where(lane < CC, 1.0, jnp.where(lane < CC + 64, right, left))


def one_hot(code):
    cell = lax.broadcasted_iota(jnp.int32, (LANES, LANES), 0).astype(F32).astype(BF)
    code = jnp.broadcast_to(code, (16, LANES)).astype(BF)
    match = cell.reshape(8, 16, LANES) == code[None]
    return jnp.where(match, jnp.ones((), BF), jnp.zeros((), BF)).reshape(LANES, LANES)


def deposit_kernel(per, last, got_ref, own, head, tail, left, right, patch_s, total):
    step = pl.program_id(0)

    @pl.when(step == 0)
    def _():
        total[...] = jnp.zeros_like(total)

    ones = jnp.ones((16, LANES), BF)

    def one(i, carry):
        meta = got_ref[i, 2 * CH :, :].astype(F32)
        for r in range(2):
            feat = jnp.concatenate([got_ref[i, r * CH : (r + 1) * CH, :], ones], axis=0)
            at = meta[2 + r, 0].astype(jnp.int32)
            patch_s[2 * (step * per + i) + r] = at
            total[at] += nt_dot(feat, one_hot(meta[r : r + 1]))
        return carry

    lax.fori_loop(0, per, one, 0, unroll=32)

    @pl.when(step == last)
    def _():
        def patch_of(a):
            value = total[a]
            return value[:CH] / (1.0 + value[CH : CH + 1])

        patches_to_rows(patch_of, own)
        write_strips(HALO_IN, own, head, tail, left, right)


SELF_PATCH = 1


def deposit(got):
    devices = got.shape[0]
    steps = 4
    per = devices // steps
    shapes = strip_shapes(HALO_IN)
    return pl.pallas_call(
        functools.partial(deposit_kernel, per, steps - 1),
        grid=(steps,),
        in_specs=[pl.BlockSpec((per, SLOT_ROWS, LANES), lambda i: (i, 0, 0))],
        out_specs=[whole(s.shape) for s in shapes] + [smem()],
        out_shape=shapes + [jax.ShapeDtypeStruct((2 * devices,), jnp.int32)],
        scratch_shapes=[pltpu.VMEM((NPATCH, CH + 16, LANES), F32)],
        compiler_params=params(),
        cost_estimate=cost(2 * 256 * 80 * 128 * 128, 6 << 20),
        name="deposit",
    )(got)


def forward_kernel(
    columns,
    rows,
    where_s,
    own,
    above,
    below,
    sides,
    above_sides,
    below_sides,
    w_in,
    w_mid,
    w_out,
    patches,
    wide,
    coarse,
    rebuilt,
    slope_in,
    slope_mid,
    fine,
    grid_out,
):
    gx, gy = where_s[0], where_s[1]
    across = column_mask(gx, columns)
    fill_wide(HALO_IN, wide, own, above, below, sides, above_sides, below_sides)

    def row_mask(row):
        at = gy * CR + row
        return jnp.where(jnp.logical_and(at >= 0, at < rows * CR), across, 0.0)

    for g in range(12):
        total = None
        for j in range(2):
            row = 2 * g + j
            pre = conv_row(wide, row, w_in[...], 1)
            value, half, square = gelu_parts(pre)
            if 4 <= row < 4 + CR:
                slope_in[row - 4] = gelu_slope(half[:, :CC], value[:, :CC], square[:, :CC])
                value = jnp.concatenate(
                    [value[:, :CC], value[:, CC:] * across[:, CC:]], axis=1
                ).astype(BF)
            else:
                value = (value * row_mask(row - 4)).astype(BF)
            fine[row] = value
            value = value.astype(F32)
            total = value if j == 0 else total + value
        coarse[g] = (0.25 * pair_sum(total)).astype(BF)

    for g in range(10):
        pre = conv_row(coarse, g, w_mid[...], 2)
        value, slope = gelu_both(pre)
        slope_mid[g] = slope
        before = coarse[g + 1].astype(F32)
        change = (before + value).astype(BF).astype(F32) - before
        for j in range(2):
            row = fine[2 * g + 2 + j].astype(F32) + change
            if 1 <= g < 9:
                rebuilt[2 * g + j, :, :CC] = row[:, :CC].astype(BF)
                rebuilt[2 * g + j, :, CC:] = (row[:, CC:] * across[:, CC:]).astype(BF)
            else:
                rebuilt[2 * g + j] = (row * row_mask(2 * g + j - 2)).astype(BF)

    for r in range(CR):
        grid_out[r] = conv_row(rebuilt, r + 1, w_out[...], 1)[:, :CC]
    for part in range(4):
        first_row, half = part // 2, part % 2
        lanes = slice(half * LANES, (half + 1) * LANES)
        found = swap_blocks([grid_out[first_row * 8 + r, :, lanes] for r in range(8)])
        for k in range(8):
            patches[first_row * 16 + half * 8 + k] = found[k].astype(BF)


def unet_forward(where, halo, w_in, w_mid, w_out, columns, rows):
    shapes = [
        jax.ShapeDtypeStruct((NPATCH, CH, LANES), BF),
        jax.ShapeDtypeStruct((CR + 2 * HALO_IN, CH, WIDE), BF),
        jax.ShapeDtypeStruct((12, CH, WIDE), BF),
        jax.ShapeDtypeStruct((20, CH, WIDE), BF),
        jax.ShapeDtypeStruct((CR, CH, CC), F32),
        jax.ShapeDtypeStruct((10, CH, WIDE), F32),
    ]
    ins = (where, *halo, w_in, w_mid, w_out)
    return pl.pallas_call(
        functools.partial(forward_kernel, columns, rows),
        in_specs=[smem()] + [vmem()] * (len(ins) - 1),
        out_specs=[vmem()] * len(shapes),
        out_shape=shapes,
        scratch_shapes=[pltpu.VMEM((24, CH, WIDE), BF), pltpu.VMEM((CR, CH, CC), F32)],
        compiler_params=params(),
        cost_estimate=cost(2 * 50 * 192 * 192 * 384, 10 << 20, 34 * CH * WIDE),
        name="unet_forward",
    )(*ins)


def share_kernel(per, patch_s, patches, out_ref):
    step = pl.program_id(0)

    def one(i, carry):
        for r in range(2):
            patch = patch_s[2 * (step * per + i) + r]
            out_ref[i, r * CH : (r + 1) * CH, :] = patches[patch]
        return carry

    lax.fori_loop(0, per, one, 0, unroll=16)


def share(patch_at, patches, devices):
    steps = 2
    per = devices // steps
    return pl.pallas_call(
        functools.partial(share_kernel, per),
        grid=(steps,),
        in_specs=[smem(), whole(patches.shape)],
        out_specs=pl.BlockSpec((per, 2 * CH, LANES), lambda i: (i, 0, 0)),
        out_shape=jax.ShapeDtypeStruct((devices, 2 * CH, LANES), BF),
        compiler_params=params(),
        cost_estimate=cost(0, 6 << 20),
        name="share",
    )(patch_at, patches)


GROUP = 16
GROUP_LANES = 2 * GROUP * LANES
PIECES = 1


def particle_kernel(
    last,
    scale,
    patch_s,
    got_ref,
    patches,
    target_ref,
    w_hidden,
    w_pred,
    w_back,
    w_grid,
    own,
    head,
    tail,
    left,
    right,
    grads,
    total,
    pair,
    errors,
):
    step = pl.program_id(0)

    @pl.when(step == 0)
    def _():
        total[...] = jnp.zeros_like(total)
        grads[...] = jnp.zeros_like(grads)

    count = GROUP // PIECES
    span = 2 * count * LANES
    grad_hidden = jnp.zeros((HID, HID), F32)
    grad_pred = jnp.zeros((CH, HID), F32)
    for piece in range(PIECES):
        whole_lanes = slice(piece * span, (piece + 1) * span)
        codes = []
        for k in range(count):
            at = piece * count + k
            meta = got_ref[at, 2 * CH :, :].astype(F32)
            for r in range(2):
                rows = slice(r * CH, (r + 1) * CH)
                start = piece * span + (2 * k + r) * LANES
                lanes = slice(start, start + LANES)
                code = meta[r : r + 1]
                patch = patch_s[2 * (step * GROUP + at) + r]
                pair[:CH, lanes] = dot(patches[patch], one_hot(code)).astype(BF)
                pair[CH:, lanes] = got_ref[at, rows, :]
                codes.append(code)
        inputs = pair[:, whole_lanes]
        hidden, slope = gelu_both(dot(w_hidden[...], inputs))
        hidden = hidden.astype(BF)
        pred = dot(w_pred[...], hidden)
        for k in range(count):
            for r in range(2):
                slot = 2 * k + r
                lanes = slice(slot * LANES, (slot + 1) * LANES)
                live = jnp.where(codes[slot] >= 0.0, scale, 0.0)
                target = target_ref[piece * count + k, r * CH : (r + 1) * CH, :].astype(F32)
                start = piece * span + slot * LANES
                errors[:, start : start + LANES] = (live * (pred[:, lanes] - target)).astype(BF)
        wrong = errors[:, whole_lanes]
        back = (dot(w_back[...], wrong) * slope).astype(BF)
        grad_hidden += nt_dot(inputs, back)
        grad_pred += nt_dot(wrong, hidden)
        given = dot(w_grid[...], back).astype(BF)
        for k in range(count):
            for r in range(2):
                slot = 2 * k + r
                patch = patch_s[2 * (step * GROUP + piece * count + k) + r]
                part = given[:, slot * LANES : (slot + 1) * LANES]
                total[patch] += nt_dot(part, one_hot(codes[slot]))
    grads[:HID] += grad_hidden
    grads[HID:] += grad_pred

    @pl.when(step == last)
    def _():
        patches_to_rows(lambda a: total[a], own)
        write_strips(HALO_OUT, own, head, tail, left, right)


def particles(patch_at, got, patches, target, w_hidden, w_pred, w_back, w_grid, scale):
    devices = got.shape[0]
    steps = devices // GROUP
    shapes = strip_shapes(HALO_OUT) + [jax.ShapeDtypeStruct((HID + CH, HID), F32)]
    return pl.pallas_call(
        functools.partial(particle_kernel, steps - 1, scale),
        grid=(steps,),
        in_specs=[
            smem(),
            pl.BlockSpec((GROUP, SLOT_ROWS, LANES), lambda i: (i, 0, 0)),
            whole(patches.shape),
            pl.BlockSpec((GROUP, 2 * CH, LANES), lambda i: (i, 0, 0)),
            whole(w_hidden.shape),
            whole(w_pred.shape),
            whole(w_back.shape),
            whole(w_grid.shape),
        ],
        out_specs=[whole(s.shape) for s in shapes],
        out_shape=shapes,
        scratch_shapes=[
            pltpu.VMEM((NPATCH, CH, LANES), F32),
            pltpu.VMEM((2 * CH, GROUP_LANES), BF),
            pltpu.VMEM((CH, GROUP_LANES), BF),
        ],
        compiler_params=params(),
        cost_estimate=cost(2 * 32768 * 128 * 700, 16 << 20, 32768 * 128),
        name="particles",
    )(patch_at, got, patches, target, w_hidden, w_pred, w_back, w_grid)


def shifted(value, shift):
    value = jnp.concatenate([value, jnp.zeros((CH, LANES), F32)], axis=1)
    return jnp.concatenate(
        [pltpu.roll(value, WIDE - shift, 1), value, pltpu.roll(value, shift, 1)], axis=0
    ).astype(BF)


def out_terms_kernel(own, rebuilt, sum_out):
    sum_out[...] = jnp.zeros_like(sum_out)

    def one(r, carry):
        sum_out[:, : 3 * CH] += nt_dot(
            rebuilt[pl.ds(r + 1, 3)].reshape(3 * CH, WIDE), shifted(own[r].astype(F32), 1)
        )
        return carry

    lax.fori_loop(0, CR, one, 0, unroll=4)


def out_terms(own, rebuilt):
    return pl.pallas_call(
        out_terms_kernel,
        in_specs=[vmem(), vmem()],
        out_specs=vmem(),
        out_shape=jax.ShapeDtypeStruct((3 * CH, 2 * LANES), F32),
        compiler_params=params(),
        cost_estimate=cost(2 * 16 * 192 * 192 * 384, 10 << 20),
        name="out_terms",
    )(own, rebuilt)


def backward_kernel(
    columns,
    rows,
    where_s,
    own,
    above,
    below,
    sides,
    above_sides,
    below_sides,
    wide_in,
    coarse,
    slope_in,
    slope_mid,
    flip_mid,
    flip_out,
    particle_grads,
    sum_out,
    staged,
    wide,
    rebuilt_grad,
    mid_grad,
    first_grad,
    sum_in,
    sum_mid,
):
    gx, gy = where_s[0], where_s[1]
    across = column_mask(gx, columns)
    fill_wide(HALO_OUT, wide, own, above, below, sides, above_sides, below_sides)

    def pooled(g, carry):
        total = None
        for j in range(2):
            value = conv_row(wide, 2 * g + j, flip_out[...], 1).astype(BF)
            rebuilt_grad[2 * g + j] = value
            value = value.astype(F32)
            total = value if j == 0 else total + value
        at = gy * CR + 2 * g - 2
        mask = jnp.where(jnp.logical_and(at >= 0, at < rows * CR), across, 0.0)
        mid_grad[g] = (pair_sum(total) * slope_mid[g] * mask).astype(BF)
        return carry

    lax.fori_loop(0, 10, pooled, 0, unroll=10)

    def fine(g, carry):
        spread = 0.25 * conv_row(mid_grad, g, flip_mid[...], 2)[:, :CC]
        for j in range(2):
            value = rebuilt_grad[2 * g + 2 + j, :, :CC].astype(F32) + spread
            first_grad[2 * g + j] = (value * slope_in[2 * g + j]).astype(BF)
        return carry

    lax.fori_loop(0, 8, fine, 0, unroll=8)

    sum_in[...] = jnp.zeros_like(sum_in)
    sum_mid[...] = jnp.zeros_like(sum_mid)

    def fine_terms(r, carry):
        sum_in[:, : 3 * CH] += nt_dot(
            wide_in[pl.ds(r + HALO_IN - 1, 3)].reshape(3 * CH, WIDE),
            shifted(first_grad[r].astype(F32), 1),
        )
        return carry

    lax.fori_loop(0, CR, fine_terms, 0, unroll=16)
    even = (lane_index((CH, CC)) & 1) == 0

    def coarse_terms(g, carry):
        value = jnp.where(even, mid_grad[g + 1, :, :CC].astype(F32), 0.0)
        sum_mid[:, : 3 * CH] += nt_dot(
            coarse[pl.ds(g + 1, 3)].reshape(3 * CH, WIDE), shifted(value, 2)
        )
        return carry

    lax.fori_loop(0, 8, coarse_terms, 0, unroll=8)

    rows_each = 3 * CH
    for which, total in enumerate((sum_in, sum_mid, sum_out)):
        for half in range(2):
            start = (2 * which + half) * rows_each
            staged[start : start + rows_each] = total[
                :, half * LANES : (half + 1) * LANES
            ].astype(BF)
    start = 6 * rows_each
    staged[start : start + HID + CH] = particle_grads[...].astype(BF)
    staged[start + HID + CH :] = jnp.zeros((REDUCE_ROWS - start - HID - CH, LANES), BF)


def unet_backward(where, halo, saved, flip_mid, flip_out, particle_grads, sum_out, columns, rows):
    ins = (where, *halo, *saved, flip_mid, flip_out, particle_grads, sum_out)
    return pl.pallas_call(
        functools.partial(backward_kernel, columns, rows),
        in_specs=[smem()] + [vmem()] * (len(ins) - 1),
        out_specs=vmem(),
        out_shape=jax.ShapeDtypeStruct((REDUCE_ROWS, LANES), BF),
        scratch_shapes=[
            pltpu.VMEM((CR + 2 * HALO_OUT, CH, WIDE), BF),
            pltpu.VMEM((20, CH, WIDE), BF),
            pltpu.VMEM((10, CH, WIDE), BF),
            pltpu.VMEM((CR, CH, CC), BF),
            pltpu.VMEM((3 * CH, 2 * LANES), F32),
            pltpu.VMEM((3 * CH, 2 * LANES), F32),
        ],
        compiler_params=params(),
        cost_estimate=cost(2 * 70 * 192 * 192 * 384, 10 << 20),
        name="unet_backward",
    )(*ins)


def split_kernel(sums, grad_in, grad_mid, grad_out, grad_grid, grad_part, grad_pred):
    for which, out in enumerate((grad_in, grad_mid, grad_out)):
        for dr in range(3):
            start = 2 * which * 3 * CH + dr * CH
            low = sums[start : start + CH, :].astype(F32)
            out[3 * dr] = low[:, :CH]
            out[3 * dr + 1] = low[:, CH:]
            out[3 * dr + 2] = sums[start + 3 * CH : start + 4 * CH, :CH].astype(F32)
    start = 18 * CH
    grad_grid[...] = sums[start : start + CH, :].astype(F32)
    grad_part[...] = sums[start + CH : start + 2 * CH, :].astype(F32)
    grad_pred[...] = sums[start + 2 * CH : start + 3 * CH, :].astype(F32)


def split(sums):
    conv = jax.ShapeDtypeStruct((9, CH, CH), F32)
    mlp = jax.ShapeDtypeStruct((CH, HID), F32)
    shapes = [conv, conv, conv, mlp, mlp, mlp]
    return pl.pallas_call(
        split_kernel,
        in_specs=[vmem()],
        out_specs=[vmem()] * 6,
        out_shape=shapes,
        compiler_params=params(),
        cost_estimate=cost(0, 3 << 20),
        name="split",
    )(sums)


def swap(value, axes=("gx", "gy")):
    return lax.all_to_all(value, axes, split_axis=0, concat_axis=0, tiled=True)


def shards(
    part_feat,
    target,
    block_tile,
    block_patch,
    cell_idx,
    block_fill,
    conv_in,
    conv_mid,
    conv_out,
    mlp_grid,
    mlp_part,
    mlp_out,
):
    nblocks = block_tile.shape[0]
    columns, rows = lax.axis_size("gx"), lax.axis_size("gy")
    devices, grid = columns * rows, (columns, rows)
    tile = block_tile[:, 0]
    where = jnp.stack([lax.axis_index("gx"), lax.axis_index("gy")]).astype(jnp.int32)
    scale = 1.0 / math.sqrt(nblocks * LANES * devices)
    w_pred = mlp_out.T
    by_row = ("gy", "gx")

    sent = dispatch(tile, block_patch, block_fill, cell_idx, part_feat, grid)
    sent_target = dispatch_target(tile, target, grid)
    got = swap(sent, by_row)
    prepared = prepare(conv_in, conv_mid, conv_out, mlp_grid, mlp_part, w_pred)
    got, sent_target, where, *prepared = lax.optimization_barrier(
        (got, sent_target, where, *prepared)
    )
    w_in, w_mid, w_out, f_mid, f_out, w_hidden, w_back = prepared
    got_target = swap(sent_target, by_row)

    own, *strips, patch_at = deposit(got)
    strips, _ = exchange(*strips)
    halo = (own, *strips)
    patches, wide_in, coarse, rebuilt, slope_in, slope_mid = unet_forward(
        where, halo, w_in, w_mid, w_out, columns, rows
    )
    got_values = swap(share(patch_at, patches, devices), by_row)
    own, *strips, particle_grads = particles(
        patch_at, got, patches, got_target, w_hidden, w_pred, w_back, mlp_grid, scale
    )
    strips, sum_out = exchange(*strips, out_terms(own, rebuilt))
    halo = (own, *strips)
    saved = (wide_in, coarse, slope_in, slope_mid)
    staged = unet_backward(
        where, halo, saved, f_mid, f_out, particle_grads, sum_out, columns, rows
    )
    staged, got_values = lax.optimization_barrier((staged, got_values))
    terms = swap(staged.reshape(devices, REDUCE_ROWS // devices, LANES))
    mine = jnp.sum(terms.astype(F32), axis=0).astype(BF)
    spread = swap(jnp.broadcast_to(mine[None], (devices, *mine.shape)))
    pred = home_predictions(
        tile, block_fill, cell_idx, got_values, part_feat, w_hidden, w_pred, grid
    )
    *grads, grad_pred = split(spread.reshape(REDUCE_ROWS, LANES))
    return (pred, *grads, grad_pred.T)


def solution(mesh):
    return jax.shard_map(
        shards,
        mesh=mesh,
        in_specs=(
            P(None, ("gx", "gy")),
            P(None, ("gx", "gy")),
            P(("gx", "gy"), None),
            P(("gx", "gy")),
            P(("gx", "gy"), None),
            P(("gx", "gy")),
            P(),
            P(),
            P(),
            P(),
            P(),
            P(),
        ),
        out_specs=(P(None, ("gx", "gy")), P(), P(), P(), P(), P(), P()),
        check_vma=False,
    )
```

```python
import functools
import math

import jax
import jax.numpy as jnp
from jax import lax
from jax.experimental import pallas as pl
from jax.experimental.pallas import tpu as pltpu
from jax.sharding import PartitionSpec as P

CH = 64
HID = 128
CR = 16
CC = 256
LANES = 128
WIDE = 384
NPATCH = 32
META = 8
SLOT_ROWS = 2 * CH + META
HALO_IN = 5
HALO_OUT = 3
REDUCE_ROWS = 2048

root_two_pi = 0.7978845608028654
cubic_coef = 0.044715

VMEM_LIMIT = 56 * 1024 * 1024
BF = jnp.bfloat16
F32 = jnp.float32


def params():
    return pltpu.CompilerParams(vmem_limit_bytes=VMEM_LIMIT)


def cost(flops, moved, tanhs=0):
    return pl.CostEstimate(flops=flops, bytes_accessed=moved, transcendentals=tanhs)


def smem():
    return pl.BlockSpec(memory_space=pltpu.SMEM)


def vmem():
    return pl.BlockSpec(memory_space=pltpu.VMEM)


def whole(shape):
    return pl.BlockSpec(shape, lambda i: (0,) * len(shape))


def nt_dot(left, right):
    return lax.dot_general(left, right, (((1,), (1,)), ((), ())), preferred_element_type=F32)


def dot(left, right):
    return jnp.dot(left, right, preferred_element_type=F32)


def gelu_both(value):
    square = value * value
    inner = jnp.tanh(value * (root_two_pi + (root_two_pi * cubic_coef) * square))
    half = 0.5 + 0.5 * inner
    result = value * half
    bend = 2.0 * root_two_pi + (6.0 * cubic_coef * root_two_pi) * square
    return result, half + (result - result * half) * bend


def gelu_slope(half, result, square):
    bend = 2.0 * root_two_pi + (6.0 * cubic_coef * root_two_pi) * square
    return half + (result - result * half) * bend


def gelu_parts(value):
    square = value * value
    inner = jnp.tanh(value * (root_two_pi + (root_two_pi * cubic_coef) * square))
    half = 0.5 + 0.5 * inner
    return value * half, half, square


def gelu_value(value):
    inner = jnp.tanh(value * (root_two_pi + (root_two_pi * cubic_coef) * (value * value)))
    return value * (0.5 + 0.5 * inner)


def lane_index(shape):
    return lax.broadcasted_iota(jnp.int32, shape, len(shape) - 1)


def peer_of(tile, grid):
    columns, rows = grid
    return lax.rem(tile, rows) * columns + lax.div(tile, rows)


def place_blocks(tile_s, slot_s, count_s, blocks, grid):
    devices = grid[0] * grid[1]

    def clear(i, carry):
        count_s[i] = 0
        slot_s[2 * i] = -1
        slot_s[2 * i + 1] = -1
        return carry

    def place(b, carry):
        owner = peer_of(tile_s[b], grid)
        rank = count_s[owner]
        slot_s[2 * owner + rank] = b
        count_s[owner] = rank + 1
        return carry

    lax.fori_loop(0, devices, clear, 0, unroll=16)
    lax.fori_loop(0, blocks, place, 0, unroll=8)


def block_lanes(b):
    return pl.ds(pl.multiple_of(b * LANES, LANES), LANES)


def dispatch_kernel(blocks, grid, per, tile_s, patch_s, fill_s, cell_ref, feat_ref, out_ref, slot_s, count_s):
    step = pl.program_id(0)

    @pl.when(step == 0)
    def _():
        place_blocks(tile_s, slot_s, count_s, blocks, grid)

    def one(i, carry):
        owner = step * per + i
        row = lax.broadcasted_iota(jnp.int32, (META, LANES), 0)
        lane = lane_index((1, LANES))
        meta = jnp.zeros((META, LANES), F32)
        for r in range(2):
            b = slot_s[2 * owner + r]
            at = jnp.maximum(b, 0)
            out_ref[i, r * CH : (r + 1) * CH, :] = feat_ref[:, block_lanes(at)]
            fill = jnp.where(b >= 0, fill_s[at], 0)
            code = jnp.where(lane < fill, cell_ref[pl.ds(at, 1), :], -1).astype(F32)
            meta = jnp.where(row == r, code, meta)
            meta = jnp.where(row == 2 + r, patch_s[at].astype(F32), meta)
        out_ref[i, 2 * CH :, :] = meta.astype(BF)
        return carry

    lax.fori_loop(0, per, one, 0, unroll=16)


def route_scratch(devices):
    return [pltpu.SMEM((2 * devices,), jnp.int32), pltpu.SMEM((devices,), jnp.int32)]


def dispatch(tile, patch, fill, cells, features, grid):
    devices = grid[0] * grid[1]
    blocks = tile.shape[0]
    steps = 2
    per = devices // steps
    return pl.pallas_call(
        functools.partial(dispatch_kernel, blocks, grid, per),
        grid=(steps,),
        in_specs=[smem(), smem(), smem(), whole(cells.shape), whole(features.shape)],
        out_specs=pl.BlockSpec((per, SLOT_ROWS, LANES), lambda i: (i, 0, 0)),
        out_shape=jax.ShapeDtypeStruct((devices, SLOT_ROWS, LANES), BF),
        scratch_shapes=route_scratch(devices),
        compiler_params=params(),
        cost_estimate=cost(0, 6 << 20),
        name="dispatch",
    )(tile, patch, fill, cells, features)


def dispatch_target_kernel(blocks, grid, per, tile_s, feat_ref, out_ref, slot_s, count_s):
    step = pl.program_id(0)

    @pl.when(step == 0)
    def _():
        place_blocks(tile_s, slot_s, count_s, blocks, grid)

    def one(i, carry):
        owner = step * per + i
        for r in range(2):
            at = jnp.maximum(slot_s[2 * owner + r], 0)
            out_ref[i, r * CH : (r + 1) * CH, :] = feat_ref[:, block_lanes(at)]
        return carry

    lax.fori_loop(0, per, one, 0, unroll=16)


def dispatch_target(tile, features, grid):
    devices = grid[0] * grid[1]
    blocks = tile.shape[0]
    steps = 4
    per = devices // steps
    return pl.pallas_call(
        functools.partial(dispatch_target_kernel, blocks, grid, per),
        grid=(steps,),
        in_specs=[smem(), whole(features.shape)],
        out_specs=pl.BlockSpec((per, 2 * CH, LANES), lambda i: (i, 0, 0)),
        out_shape=jax.ShapeDtypeStruct((devices, 2 * CH, LANES), BF),
        scratch_shapes=route_scratch(devices),
        compiler_params=params(),
        cost_estimate=cost(0, 6 << 20),
        name="dispatch_target",
    )(tile, features)


def home_kernel(blocks, grid, tile_s, fill_s, cell_ref, got_ref, feat_ref, w_hidden, w_pred, out_ref, pair, count_s):
    def clear(i, carry):
        count_s[i] = 0
        return carry

    lax.fori_loop(0, grid[0] * grid[1], clear, 0, unroll=16)

    def one(b, carry):
        owner = peer_of(tile_s[b], grid)
        rank = count_s[owner]
        count_s[owner] = rank + 1
        rows = pl.ds(pl.multiple_of(rank * CH, CH), CH)
        code = jnp.where(lane_index((1, LANES)) < fill_s[b], cell_ref[pl.ds(b, 1), :], -1)
        values = dot(got_ref[owner, rows, :], one_hot(code.astype(F32)))
        pair[:CH, block_lanes(b)] = values.astype(BF)
        return carry

    lax.fori_loop(0, blocks, one, 0, unroll=16)
    pair[CH:, :] = feat_ref[...]
    span = 2048
    for start in range(0, blocks * LANES, span):
        lanes = slice(start, start + span)
        value = gelu_value(dot(w_hidden[...], pair[:, lanes])).astype(BF)
        out_ref[:, lanes] = dot(w_pred[...], value).astype(BF)


def home_predictions(tile, fill, cells, got, features, w_hidden, w_pred, grid):
    devices = grid[0] * grid[1]
    blocks = tile.shape[0]
    return pl.pallas_call(
        functools.partial(home_kernel, blocks, grid),
        in_specs=[smem(), smem()] + [vmem()] * 5,
        out_specs=vmem(),
        out_shape=jax.ShapeDtypeStruct((CH, blocks * LANES), BF),
        scratch_shapes=[
            pltpu.VMEM((2 * CH, blocks * LANES), BF),
            pltpu.SMEM((devices,), jnp.int32),
        ],
        compiler_params=params(),
        cost_estimate=cost(2 * 8192 * 128 * 192, 8 << 20, 8192 * 128),
        name="home_predictions",
    )(tile, fill, cells, got, features, w_hidden, w_pred)


def prepare_kernel(conv_in, conv_mid, conv_out, mlp_grid, mlp_part, mlp_out_t, w_in, w_mid, w_out, f_mid, f_out, w_hidden, w_back):
    for conv, out, flip in ((conv_in, w_in, None), (conv_mid, w_mid, f_mid), (conv_out, w_out, f_out)):
        for dr in range(3):
            for dq in range(3):
                rows = slice(dq * CH, (dq + 1) * CH)
                lanes = slice(dr * CH, (dr + 1) * CH)
                out[rows, lanes] = conv[3 * dr + dq].astype(F32).T.astype(BF)
                if flip is not None:
                    flip[rows, lanes] = conv[8 - 3 * dr - dq]
    w_hidden[:, :CH] = mlp_grid[...].astype(F32).T.astype(BF)
    w_hidden[:, CH:] = mlp_part[...].astype(F32).T.astype(BF)
    w_back[...] = mlp_out_t[...].astype(F32).T.astype(BF)


def prepare(*weights):
    square = jax.ShapeDtypeStruct((3 * CH, 3 * CH), BF)
    shapes = [square] * 5 + [
        jax.ShapeDtypeStruct((HID, 2 * CH), BF),
        jax.ShapeDtypeStruct((HID, CH), BF),
    ]
    return pl.pallas_call(
        prepare_kernel,
        in_specs=[vmem()] * len(weights),
        out_specs=[vmem()] * len(shapes),
        out_shape=shapes,
        compiler_params=params(),
        cost_estimate=cost(0, 1 << 20),
        name="prepare",
    )(*weights)


def swap_blocks(parts):
    parts = list(parts)
    group = lane_index(parts[0].shape) // 16
    for s in (4, 2, 1):
        keep = (group & s) == 0
        for i in range(8):
            if i & s:
                continue
            a, b = parts[i], parts[i + s]
            parts[i] = jnp.where(keep, a, pltpu.roll(b, s * 16, 1))
            parts[i + s] = jnp.where(keep, pltpu.roll(a, LANES - s * 16, 1), b)
    return parts


def patches_to_rows(patch_of, own_ref):
    for part in range(4):
        first, half = part // 2, part % 2
        rows = swap_blocks([patch_of(first * 16 + half * 8 + k) for k in range(8)])
        for r in range(8):
            own_ref[first * 8 + r, :, half * LANES : (half + 1) * LANES] = rows[r].astype(BF)


def write_strips(width, own_ref, head_ref, tail_ref, left_ref, right_ref):
    for r in range(width):
        for half in range(2):
            lanes = slice(half * LANES, (half + 1) * LANES)
            head_ref[2 * r + half] = own_ref[r, :, lanes]
            tail_ref[2 * r + half] = own_ref[CR - width + r, :, lanes]
    group = lane_index((CH, LANES)) // 8
    left = jnp.zeros((CH, LANES), F32)
    right = jnp.zeros((CH, LANES), F32)
    for r in range(CR):
        piece = own_ref[r, :, :LANES].astype(F32)
        left = jnp.where(group == r, pltpu.roll(piece, 8 * r, 1) if r else piece, left)
        piece = own_ref[r, :, LANES:].astype(F32)
        turn = (8 * r + 8) % LANES
        right = jnp.where(group == r, pltpu.roll(piece, turn, 1) if turn else piece, right)
    left_ref[0] = left.astype(BF)
    right_ref[0] = right.astype(BF)


def strip_shapes(width):
    return [
        jax.ShapeDtypeStruct((CR, CH, CC), BF),
        jax.ShapeDtypeStruct((2 * width, CH, LANES), BF),
        jax.ShapeDtypeStruct((2 * width, CH, LANES), BF),
        jax.ShapeDtypeStruct((1, CH, LANES), BF),
        jax.ShapeDtypeStruct((1, CH, LANES), BF),
    ]


def ahead(value, axis):
    count = lax.axis_size(axis)
    return lax.ppermute(value, axis, [(i, i + 1) for i in range(count - 1)])


def behind(value, axis):
    count = lax.axis_size(axis)
    return lax.ppermute(value, axis, [(i + 1, i) for i in range(count - 1)])


def exchange(head, tail, left, right, beside=None):
    from_left, from_right = ahead(right, "gx"), behind(left, "gx")
    above, below = ahead(tail, "gy"), behind(head, "gy")
    if beside is not None:
        from_left, from_right, beside = lax.optimization_barrier((from_left, from_right, beside))
    sides = jnp.concatenate([from_left, from_right], axis=0)
    return (above, below, sides, ahead(sides, "gy"), behind(sides, "gy")), beside


def side_lanes(left, right, r):
    lane = lane_index((CH, LANES))
    turn_right = (LANES - 8 * r) % LANES
    turn_left = (120 - 8 * r) % LANES
    right = pltpu.roll(right, turn_right, 1) if turn_right else right
    left = pltpu.roll(left, turn_left, 1) if turn_left else left
    return jnp.where(lane < 8, right, jnp.where(lane >= 120, left, 0.0)).astype(BF)


def fill_wide(width, wide, own_ref, above_ref, below_ref, sides, above_sides, below_sides):
    left, right = sides[0].astype(F32), sides[1].astype(F32)
    for r in range(CR):
        wide[width + r, :, :CC] = own_ref[r]
        wide[width + r, :, CC:] = side_lanes(left, right, r)
    left, right = above_sides[0].astype(F32), above_sides[1].astype(F32)
    for r in range(width):
        wide[r, :, :LANES] = above_ref[2 * r]
        wide[r, :, LANES:CC] = above_ref[2 * r + 1]
        wide[r, :, CC:] = side_lanes(left, right, CR - width + r)
    left, right = below_sides[0].astype(F32), below_sides[1].astype(F32)
    for r in range(width):
        at = width + CR + r
        wide[at, :, :LANES] = below_ref[2 * r]
        wide[at, :, LANES:CC] = below_ref[2 * r + 1]
        wide[at, :, CC:] = side_lanes(left, right, r)


def conv_row(source, at, weight, shift):
    stacked = source[pl.ds(at, 3)].reshape(3 * CH, WIDE)
    terms = dot(weight, stacked)
    return (
        terms[CH : 2 * CH]
        + pltpu.roll(terms[:CH], shift, 1)
        + pltpu.roll(terms[2 * CH :], WIDE - shift, 1)
    )


def pair_sum(value):
    even = (lane_index(value.shape) & 1) == 0
    return value + jnp.where(even, pltpu.roll(value, WIDE - 1, 1), pltpu.roll(value, 1, 1))


def column_mask(gx, columns):
    lane = lane_index((1, WIDE))
    right = jnp.where(gx < columns - 1, 1.0, 0.0)
    left = jnp.where(gx > 0, 1.0, 0.0)
    return jnp.where(lane < CC, 1.0, jnp.where(lane < CC + 64, right, left))


def one_hot(code):
    cell = lax.broadcasted_iota(jnp.int32, (LANES, LANES), 0).astype(F32).astype(BF)
    code = jnp.broadcast_to(code, (16, LANES)).astype(BF)
    match = cell.reshape(8, 16, LANES) == code[None]
    return jnp.where(match, jnp.ones((), BF), jnp.zeros((), BF)).reshape(LANES, LANES)


def deposit_kernel(per, last, got_ref, own, head, tail, left, right, patch_s, total):
    step = pl.program_id(0)

    @pl.when(step == 0)
    def _():
        total[...] = jnp.zeros_like(total)

    ones = jnp.ones((16, LANES), BF)

    def one(i, carry):
        meta = got_ref[i, 2 * CH :, :].astype(F32)
        for r in range(2):
            feat = jnp.concatenate([got_ref[i, r * CH : (r + 1) * CH, :], ones], axis=0)
            at = meta[2 + r, 0].astype(jnp.int32)
            patch_s[2 * (step * per + i) + r] = at
            total[at] += nt_dot(feat, one_hot(meta[r : r + 1]))
        return carry

    lax.fori_loop(0, per, one, 0, unroll=32)

    @pl.when(step == last)
    def _():
        def patch_of(a):
            value = total[a]
            return value[:CH] / (1.0 + value[CH : CH + 1])

        patches_to_rows(patch_of, own)
        write_strips(HALO_IN, own, head, tail, left, right)


SELF_PATCH = 1


def deposit(got):
    devices = got.shape[0]
    steps = 4
    per = devices // steps
    shapes = strip_shapes(HALO_IN)
    return pl.pallas_call(
        functools.partial(deposit_kernel, per, steps - 1),
        grid=(steps,),
        in_specs=[pl.BlockSpec((per, SLOT_ROWS, LANES), lambda i: (i, 0, 0))],
        out_specs=[whole(s.shape) for s in shapes] + [smem()],
        out_shape=shapes + [jax.ShapeDtypeStruct((2 * devices,), jnp.int32)],
        scratch_shapes=[pltpu.VMEM((NPATCH, CH + 16, LANES), F32)],
        compiler_params=params(),
        cost_estimate=cost(2 * 256 * 80 * 128 * 128, 6 << 20),
        name="deposit",
    )(got)


def forward_kernel(
    columns,
    rows,
    where_s,
    own,
    above,
    below,
    sides,
    above_sides,
    below_sides,
    w_in,
    w_mid,
    w_out,
    patches,
    wide,
    coarse,
    rebuilt,
    slope_in,
    slope_mid,
    fine,
    grid_out,
):
    gx, gy = where_s[0], where_s[1]
    across = column_mask(gx, columns)
    fill_wide(HALO_IN, wide, own, above, below, sides, above_sides, below_sides)

    def row_mask(row):
        at = gy * CR + row
        return jnp.where(jnp.logical_and(at >= 0, at < rows * CR), across, 0.0)

    for g in range(12):
        total = None
        for j in range(2):
            row = 2 * g + j
            pre = conv_row(wide, row, w_in[...], 1)
            value, half, square = gelu_parts(pre)
            if 4 <= row < 4 + CR:
                slope_in[row - 4] = gelu_slope(half[:, :CC], value[:, :CC], square[:, :CC])
                value = jnp.concatenate(
                    [value[:, :CC], value[:, CC:] * across[:, CC:]], axis=1
                ).astype(BF)
            else:
                value = (value * row_mask(row - 4)).astype(BF)
            fine[row] = value
            value = value.astype(F32)
            total = value if j == 0 else total + value
        coarse[g] = (0.25 * pair_sum(total)).astype(BF)

    for g in range(10):
        pre = conv_row(coarse, g, w_mid[...], 2)
        value, slope = gelu_both(pre)
        slope_mid[g] = slope
        before = coarse[g + 1].astype(F32)
        change = (before + value).astype(BF).astype(F32) - before
        for j in range(2):
            row = fine[2 * g + 2 + j].astype(F32) + change
            if 1 <= g < 9:
                rebuilt[2 * g + j, :, :CC] = row[:, :CC].astype(BF)
                rebuilt[2 * g + j, :, CC:] = (row[:, CC:] * across[:, CC:]).astype(BF)
            else:
                rebuilt[2 * g + j] = (row * row_mask(2 * g + j - 2)).astype(BF)

    for r in range(CR):
        grid_out[r] = conv_row(rebuilt, r + 1, w_out[...], 1)[:, :CC]
    for part in range(4):
        first_row, half = part // 2, part % 2
        lanes = slice(half * LANES, (half + 1) * LANES)
        found = swap_blocks([grid_out[first_row * 8 + r, :, lanes] for r in range(8)])
        for k in range(8):
            patches[first_row * 16 + half * 8 + k] = found[k].astype(BF)


def unet_forward(where, halo, w_in, w_mid, w_out, columns, rows):
    shapes = [
        jax.ShapeDtypeStruct((NPATCH, CH, LANES), BF),
        jax.ShapeDtypeStruct((CR + 2 * HALO_IN, CH, WIDE), BF),
        jax.ShapeDtypeStruct((12, CH, WIDE), BF),
        jax.ShapeDtypeStruct((20, CH, WIDE), BF),
        jax.ShapeDtypeStruct((CR, CH, CC), F32),
        jax.ShapeDtypeStruct((10, CH, WIDE), F32),
    ]
    ins = (where, *halo, w_in, w_mid, w_out)
    return pl.pallas_call(
        functools.partial(forward_kernel, columns, rows),
        in_specs=[smem()] + [vmem()] * (len(ins) - 1),
        out_specs=[vmem()] * len(shapes),
        out_shape=shapes,
        scratch_shapes=[pltpu.VMEM((24, CH, WIDE), BF), pltpu.VMEM((CR, CH, CC), F32)],
        compiler_params=params(),
        cost_estimate=cost(2 * 50 * 192 * 192 * 384, 10 << 20, 34 * CH * WIDE),
        name="unet_forward",
    )(*ins)


def share_kernel(per, patch_s, patches, out_ref):
    step = pl.program_id(0)

    def one(i, carry):
        for r in range(2):
            patch = patch_s[2 * (step * per + i) + r]
            out_ref[i, r * CH : (r + 1) * CH, :] = patches[patch]
        return carry

    lax.fori_loop(0, per, one, 0, unroll=16)


def share(patch_at, patches, devices):
    steps = 2
    per = devices // steps
    return pl.pallas_call(
        functools.partial(share_kernel, per),
        grid=(steps,),
        in_specs=[smem(), whole(patches.shape)],
        out_specs=pl.BlockSpec((per, 2 * CH, LANES), lambda i: (i, 0, 0)),
        out_shape=jax.ShapeDtypeStruct((devices, 2 * CH, LANES), BF),
        compiler_params=params(),
        cost_estimate=cost(0, 6 << 20),
        name="share",
    )(patch_at, patches)


GROUP = 16
GROUP_LANES = 2 * GROUP * LANES
PIECES = 1


def particle_kernel(
    last,
    scale,
    patch_s,
    got_ref,
    patches,
    target_ref,
    w_hidden,
    w_pred,
    w_back,
    w_grid,
    own,
    head,
    tail,
    left,
    right,
    grads,
    total,
    pair,
    errors,
):
    step = pl.program_id(0)

    @pl.when(step == 0)
    def _():
        total[...] = jnp.zeros_like(total)
        grads[...] = jnp.zeros_like(grads)

    count = GROUP // PIECES
    span = 2 * count * LANES
    grad_hidden = jnp.zeros((HID, HID), F32)
    grad_pred = jnp.zeros((CH, HID), F32)
    for piece in range(PIECES):
        whole_lanes = slice(piece * span, (piece + 1) * span)
        codes = []
        for k in range(count):
            at = piece * count + k
            meta = got_ref[at, 2 * CH :, :].astype(F32)
            for r in range(2):
                rows = slice(r * CH, (r + 1) * CH)
                start = piece * span + (2 * k + r) * LANES
                lanes = slice(start, start + LANES)
                code = meta[r : r + 1]
                patch = patch_s[2 * (step * GROUP + at) + r]
                pair[:CH, lanes] = dot(patches[patch], one_hot(code)).astype(BF)
                pair[CH:, lanes] = got_ref[at, rows, :]
                codes.append(code)
        inputs = pair[:, whole_lanes]
        hidden, slope = gelu_both(dot(w_hidden[...], inputs))
        hidden = hidden.astype(BF)
        pred = dot(w_pred[...], hidden)
        for k in range(count):
            for r in range(2):
                slot = 2 * k + r
                lanes = slice(slot * LANES, (slot + 1) * LANES)
                live = jnp.where(codes[slot] >= 0.0, scale, 0.0)
                target = target_ref[piece * count + k, r * CH : (r + 1) * CH, :].astype(F32)
                start = piece * span + slot * LANES
                errors[:, start : start + LANES] = (live * (pred[:, lanes] - target)).astype(BF)
        wrong = errors[:, whole_lanes]
        back = (dot(w_back[...], wrong) * slope).astype(BF)
        grad_hidden += nt_dot(inputs, back)
        grad_pred += nt_dot(wrong, hidden)
        given = dot(w_grid[...], back).astype(BF)
        for k in range(count):
            for r in range(2):
                slot = 2 * k + r
                patch = patch_s[2 * (step * GROUP + piece * count + k) + r]
                part = given[:, slot * LANES : (slot + 1) * LANES]
                total[patch] += nt_dot(part, one_hot(codes[slot]))
    grads[:HID] += grad_hidden
    grads[HID:] += grad_pred

    @pl.when(step == last)
    def _():
        patches_to_rows(lambda a: total[a], own)
        write_strips(HALO_OUT, own, head, tail, left, right)


def particles(patch_at, got, patches, target, w_hidden, w_pred, w_back, w_grid, scale):
    devices = got.shape[0]
    steps = devices // GROUP
    shapes = strip_shapes(HALO_OUT) + [jax.ShapeDtypeStruct((HID + CH, HID), F32)]
    return pl.pallas_call(
        functools.partial(particle_kernel, steps - 1, scale),
        grid=(steps,),
        in_specs=[
            smem(),
            pl.BlockSpec((GROUP, SLOT_ROWS, LANES), lambda i: (i, 0, 0)),
            whole(patches.shape),
            pl.BlockSpec((GROUP, 2 * CH, LANES), lambda i: (i, 0, 0)),
            whole(w_hidden.shape),
            whole(w_pred.shape),
            whole(w_back.shape),
            whole(w_grid.shape),
        ],
        out_specs=[whole(s.shape) for s in shapes],
        out_shape=shapes,
        scratch_shapes=[
            pltpu.VMEM((NPATCH, CH, LANES), F32),
            pltpu.VMEM((2 * CH, GROUP_LANES), BF),
            pltpu.VMEM((CH, GROUP_LANES), BF),
        ],
        compiler_params=params(),
        cost_estimate=cost(2 * 32768 * 128 * 700, 16 << 20, 32768 * 128),
        name="particles",
    )(patch_at, got, patches, target, w_hidden, w_pred, w_back, w_grid)


def shifted(value, shift):
    value = jnp.concatenate([value, jnp.zeros((CH, LANES), F32)], axis=1)
    return jnp.concatenate(
        [pltpu.roll(value, WIDE - shift, 1), value, pltpu.roll(value, shift, 1)], axis=0
    ).astype(BF)


def out_terms_kernel(start, own, rebuilt, sum_out):
    sum_out[...] = jnp.zeros_like(sum_out)
    for r in range(start, start + CR // 2):
        sum_out[:, : 3 * CH] += nt_dot(
            rebuilt[r + 1 : r + 4].reshape(3 * CH, WIDE), shifted(own[r].astype(F32), 1)
        )


def out_terms(own, rebuilt, start):
    return pl.pallas_call(
        functools.partial(out_terms_kernel, start),
        in_specs=[vmem(), vmem()],
        out_specs=vmem(),
        out_shape=jax.ShapeDtypeStruct((3 * CH, 2 * LANES), F32),
        compiler_params=params(),
        cost_estimate=cost(2 * 8 * 192 * 192 * 384, 5 << 20),
        name="out_terms",
    )(own, rebuilt)


def backward_kernel(
    columns,
    rows,
    where_s,
    own,
    above,
    below,
    sides,
    above_sides,
    below_sides,
    wide_in,
    coarse,
    slope_in,
    slope_mid,
    flip_mid,
    flip_out,
    particle_grads,
    upper_out,
    lower_out,
    staged,
    wide,
    rebuilt_grad,
    mid_grad,
    first_grad,
    sum_in,
    sum_mid,
):
    gx, gy = where_s[0], where_s[1]
    across = column_mask(gx, columns)
    fill_wide(HALO_OUT, wide, own, above, below, sides, above_sides, below_sides)

    def pooled(g, carry):
        total = None
        for j in range(2):
            value = conv_row(wide, 2 * g + j, flip_out[...], 1).astype(BF)
            rebuilt_grad[2 * g + j] = value
            value = value.astype(F32)
            total = value if j == 0 else total + value
        at = gy * CR + 2 * g - 2
        mask = jnp.where(jnp.logical_and(at >= 0, at < rows * CR), across, 0.0)
        mid_grad[g] = (pair_sum(total) * slope_mid[g] * mask).astype(BF)
        return carry

    lax.fori_loop(0, 10, pooled, 0, unroll=10)

    def fine(g, carry):
        spread = 0.25 * conv_row(mid_grad, g, flip_mid[...], 2)[:, :CC]
        for j in range(2):
            value = rebuilt_grad[2 * g + 2 + j, :, :CC].astype(F32) + spread
            first_grad[2 * g + j] = (value * slope_in[2 * g + j]).astype(BF)
        return carry

    lax.fori_loop(0, 8, fine, 0, unroll=8)

    sum_in[...] = jnp.zeros_like(sum_in)
    sum_mid[...] = jnp.zeros_like(sum_mid)

    def fine_terms(r, carry):
        sum_in[:, : 3 * CH] += nt_dot(
            wide_in[pl.ds(r + HALO_IN - 1, 3)].reshape(3 * CH, WIDE),
            shifted(first_grad[r].astype(F32), 1),
        )
        return carry

    lax.fori_loop(0, CR, fine_terms, 0, unroll=16)
    even = (lane_index((CH, CC)) & 1) == 0

    def coarse_terms(g, carry):
        value = jnp.where(even, mid_grad[g + 1, :, :CC].astype(F32), 0.0)
        sum_mid[:, : 3 * CH] += nt_dot(
            coarse[pl.ds(g + 1, 3)].reshape(3 * CH, WIDE), shifted(value, 2)
        )
        return carry

    lax.fori_loop(0, 8, coarse_terms, 0, unroll=8)

    rows_each = 3 * CH
    for which, total in enumerate(((sum_in,), (sum_mid,), (upper_out, lower_out))):
        for half in range(2):
            start = (2 * which + half) * rows_each
            lanes = slice(half * LANES, (half + 1) * LANES)
            staged[start : start + rows_each] = sum(part[:, lanes] for part in total).astype(BF)
    start = 6 * rows_each
    staged[start : start + HID + CH] = particle_grads[...].astype(BF)
    staged[start + HID + CH :] = jnp.zeros((REDUCE_ROWS - start - HID - CH, LANES), BF)


def unet_backward(where, halo, saved, flip_mid, flip_out, particle_grads, sums_out, columns, rows):
    ins = (where, *halo, *saved, flip_mid, flip_out, particle_grads, *sums_out)
    return pl.pallas_call(
        functools.partial(backward_kernel, columns, rows),
        in_specs=[smem()] + [vmem()] * (len(ins) - 1),
        out_specs=vmem(),
        out_shape=jax.ShapeDtypeStruct((REDUCE_ROWS, LANES), BF),
        scratch_shapes=[
            pltpu.VMEM((CR + 2 * HALO_OUT, CH, WIDE), BF),
            pltpu.VMEM((20, CH, WIDE), BF),
            pltpu.VMEM((10, CH, WIDE), BF),
            pltpu.VMEM((CR, CH, CC), BF),
            pltpu.VMEM((3 * CH, 2 * LANES), F32),
            pltpu.VMEM((3 * CH, 2 * LANES), F32),
        ],
        compiler_params=params(),
        cost_estimate=cost(2 * 70 * 192 * 192 * 384, 10 << 20),
        name="unet_backward",
    )(*ins)


def split_kernel(sums, grad_in, grad_mid, grad_out, grad_grid, grad_part, grad_pred):
    for which, out in enumerate((grad_in, grad_mid, grad_out)):
        for dr in range(3):
            start = 2 * which * 3 * CH + dr * CH
            low = sums[start : start + CH, :].astype(F32)
            out[3 * dr] = low[:, :CH]
            out[3 * dr + 1] = low[:, CH:]
            out[3 * dr + 2] = sums[start + 3 * CH : start + 4 * CH, :CH].astype(F32)
    start = 18 * CH
    grad_grid[...] = sums[start : start + CH, :].astype(F32)
    grad_part[...] = sums[start + CH : start + 2 * CH, :].astype(F32)
    grad_pred[...] = sums[start + 2 * CH : start + 3 * CH, :].astype(F32)


def split(sums):
    conv = jax.ShapeDtypeStruct((9, CH, CH), F32)
    mlp = jax.ShapeDtypeStruct((CH, HID), F32)
    shapes = [conv, conv, conv, mlp, mlp, mlp]
    return pl.pallas_call(
        split_kernel,
        in_specs=[vmem()],
        out_specs=[vmem()] * 6,
        out_shape=shapes,
        compiler_params=params(),
        cost_estimate=cost(0, 3 << 20),
        name="split",
    )(sums)


def swap(value, axes=("gx", "gy")):
    return lax.all_to_all(value, axes, split_axis=0, concat_axis=0, tiled=True)


def shards(
    part_feat,
    target,
    block_tile,
    block_patch,
    cell_idx,
    block_fill,
    conv_in,
    conv_mid,
    conv_out,
    mlp_grid,
    mlp_part,
    mlp_out,
):
    nblocks = block_tile.shape[0]
    columns, rows = lax.axis_size("gx"), lax.axis_size("gy")
    devices, grid = columns * rows, (columns, rows)
    tile = block_tile[:, 0]
    where = jnp.stack([lax.axis_index("gx"), lax.axis_index("gy")]).astype(jnp.int32)
    scale = 1.0 / math.sqrt(nblocks * LANES * devices)
    w_pred = mlp_out.T
    by_row = ("gy", "gx")

    sent = dispatch(tile, block_patch, block_fill, cell_idx, part_feat, grid)
    sent_target = dispatch_target(tile, target, grid)
    got = swap(sent, by_row)
    prepared = prepare(conv_in, conv_mid, conv_out, mlp_grid, mlp_part, w_pred)
    got, sent_target, where, *prepared = lax.optimization_barrier(
        (got, sent_target, where, *prepared)
    )
    w_in, w_mid, w_out, f_mid, f_out, w_hidden, w_back = prepared
    got_target = swap(sent_target, by_row)

    own, *strips, patch_at = deposit(got)
    strips, _ = exchange(*strips)
    halo = (own, *strips)
    patches, wide_in, coarse, rebuilt, slope_in, slope_mid = unet_forward(
        where, halo, w_in, w_mid, w_out, columns, rows
    )
    got_values = swap(share(patch_at, patches, devices), by_row)
    own, *strips, particle_grads = particles(
        patch_at, got, patches, got_target, w_hidden, w_pred, w_back, mlp_grid, scale
    )
    strips, upper_out = exchange(*strips, out_terms(own, rebuilt, 0))
    sums_out = (upper_out, out_terms(own, rebuilt, CR // 2))
    halo = (own, *strips)
    saved = (wide_in, coarse, slope_in, slope_mid)
    staged = unet_backward(
        where, halo, saved, f_mid, f_out, particle_grads, sums_out, columns, rows
    )
    staged, got_values = lax.optimization_barrier((staged, got_values))
    terms = swap(staged.reshape(devices, REDUCE_ROWS // devices, LANES))
    mine = jnp.sum(terms.astype(F32), axis=0).astype(BF)
    spread = swap(jnp.broadcast_to(mine[None], (devices, *mine.shape)))
    pred = home_predictions(
        tile, block_fill, cell_idx, got_values, part_feat, w_hidden, w_pred, grid
    )
    *grads, grad_pred = split(spread.reshape(REDUCE_ROWS, LANES))
    return (pred, *grads, grad_pred.T)


def solution(mesh):
    return jax.shard_map(
        shards,
        mesh=mesh,
        in_specs=(
            P(None, ("gx", "gy")),
            P(None, ("gx", "gy")),
            P(("gx", "gy"), None),
            P(("gx", "gy")),
            P(("gx", "gy"), None),
            P(("gx", "gy")),
            P(),
            P(),
            P(),
            P(),
            P(),
            P(),
        ),
        out_specs=(P(None, ("gx", "gy")), P(), P(), P(), P(), P(), P()),
        check_vma=False,
    )
```

```python
import functools
import math

import jax
import jax.numpy as jnp
from jax import lax
from jax.experimental import pallas as pl
from jax.experimental.pallas import tpu as pltpu
from jax.sharding import PartitionSpec as P

CH = 64
HID = 128
CR = 16
CC = 256
LANES = 128
WIDE = 384
NPATCH = 32
META = 8
SLOT_ROWS = 2 * CH + META
HALO_IN = 5
HALO_OUT = 3
REDUCE_ROWS = 2048

root_two_pi = 0.7978845608028654
cubic_coef = 0.044715

VMEM_LIMIT = 56 * 1024 * 1024
BF = jnp.bfloat16
F32 = jnp.float32


def params():
    return pltpu.CompilerParams(vmem_limit_bytes=VMEM_LIMIT)


def cost(flops, moved, tanhs=0):
    return pl.CostEstimate(flops=flops, bytes_accessed=moved, transcendentals=tanhs)


def smem():
    return pl.BlockSpec(memory_space=pltpu.SMEM)


def vmem():
    return pl.BlockSpec(memory_space=pltpu.VMEM)


def whole(shape):
    return pl.BlockSpec(shape, lambda i: (0,) * len(shape))


def nt_dot(left, right):
    return lax.dot_general(left, right, (((1,), (1,)), ((), ())), preferred_element_type=F32)


def dot(left, right):
    return jnp.dot(left, right, preferred_element_type=F32)


def gelu_both(value):
    square = value * value
    inner = jnp.tanh(value * (root_two_pi + (root_two_pi * cubic_coef) * square))
    half = 0.5 + 0.5 * inner
    result = value * half
    bend = 2.0 * root_two_pi + (6.0 * cubic_coef * root_two_pi) * square
    return result, half + (result - result * half) * bend


def gelu_slope(half, result, square):
    bend = 2.0 * root_two_pi + (6.0 * cubic_coef * root_two_pi) * square
    return half + (result - result * half) * bend


def gelu_parts(value):
    square = value * value
    inner = jnp.tanh(value * (root_two_pi + (root_two_pi * cubic_coef) * square))
    half = 0.5 + 0.5 * inner
    return value * half, half, square


def gelu_value(value):
    inner = jnp.tanh(value * (root_two_pi + (root_two_pi * cubic_coef) * (value * value)))
    return value * (0.5 + 0.5 * inner)


def lane_index(shape):
    return lax.broadcasted_iota(jnp.int32, shape, len(shape) - 1)


def peer_of(tile, grid):
    columns, rows = grid
    return lax.rem(tile, rows) * columns + lax.div(tile, rows)


def place_blocks(tile_s, slot_s, count_s, blocks, grid):
    devices = grid[0] * grid[1]

    def clear(i, carry):
        count_s[i] = 0
        slot_s[2 * i] = -1
        slot_s[2 * i + 1] = -1
        return carry

    def place(b, carry):
        owner = peer_of(tile_s[b], grid)
        rank = count_s[owner]
        slot_s[2 * owner + rank] = b
        count_s[owner] = rank + 1
        return carry

    lax.fori_loop(0, devices, clear, 0, unroll=16)
    lax.fori_loop(0, blocks, place, 0, unroll=8)


def block_lanes(b):
    return pl.ds(pl.multiple_of(b * LANES, LANES), LANES)


def dispatch_kernel(blocks, grid, per, tile_s, patch_s, fill_s, cell_ref, feat_ref, out_ref, slot_s, count_s):
    step = pl.program_id(0)

    @pl.when(step == 0)
    def _():
        place_blocks(tile_s, slot_s, count_s, blocks, grid)

    def one(i, carry):
        owner = step * per + i
        row = lax.broadcasted_iota(jnp.int32, (META, LANES), 0)
        lane = lane_index((1, LANES))
        meta = jnp.zeros((META, LANES), F32)
        for r in range(2):
            b = slot_s[2 * owner + r]
            at = jnp.maximum(b, 0)
            out_ref[i, r * CH : (r + 1) * CH, :] = feat_ref[:, block_lanes(at)]
            fill = jnp.where(b >= 0, fill_s[at], 0)
            code = jnp.where(lane < fill, cell_ref[pl.ds(at, 1), :], -1).astype(F32)
            meta = jnp.where(row == r, code, meta)
            meta = jnp.where(row == 2 + r, patch_s[at].astype(F32), meta)
        out_ref[i, 2 * CH :, :] = meta.astype(BF)
        return carry

    lax.fori_loop(0, per, one, 0, unroll=16)


def route_scratch(devices):
    return [pltpu.SMEM((2 * devices,), jnp.int32), pltpu.SMEM((devices,), jnp.int32)]


def dispatch(tile, patch, fill, cells, features, grid):
    devices = grid[0] * grid[1]
    blocks = tile.shape[0]
    steps = 2
    per = devices // steps
    return pl.pallas_call(
        functools.partial(dispatch_kernel, blocks, grid, per),
        grid=(steps,),
        in_specs=[smem(), smem(), smem(), whole(cells.shape), whole(features.shape)],
        out_specs=pl.BlockSpec((per, SLOT_ROWS, LANES), lambda i: (i, 0, 0)),
        out_shape=jax.ShapeDtypeStruct((devices, SLOT_ROWS, LANES), BF),
        scratch_shapes=route_scratch(devices),
        compiler_params=params(),
        cost_estimate=cost(0, 6 << 20),
        name="dispatch",
    )(tile, patch, fill, cells, features)


def dispatch_target_kernel(blocks, grid, per, tile_s, feat_ref, out_ref, slot_s, count_s):
    step = pl.program_id(0)

    @pl.when(step == 0)
    def _():
        place_blocks(tile_s, slot_s, count_s, blocks, grid)

    def one(i, carry):
        owner = step * per + i
        for r in range(2):
            at = jnp.maximum(slot_s[2 * owner + r], 0)
            out_ref[i, r * CH : (r + 1) * CH, :] = feat_ref[:, block_lanes(at)]
        return carry

    lax.fori_loop(0, per, one, 0, unroll=16)


def dispatch_target(tile, features, grid):
    devices = grid[0] * grid[1]
    blocks = tile.shape[0]
    steps = 4
    per = devices // steps
    return pl.pallas_call(
        functools.partial(dispatch_target_kernel, blocks, grid, per),
        grid=(steps,),
        in_specs=[smem(), whole(features.shape)],
        out_specs=pl.BlockSpec((per, 2 * CH, LANES), lambda i: (i, 0, 0)),
        out_shape=jax.ShapeDtypeStruct((devices, 2 * CH, LANES), BF),
        scratch_shapes=route_scratch(devices),
        compiler_params=params(),
        cost_estimate=cost(0, 6 << 20),
        name="dispatch_target",
    )(tile, features)


def home_kernel(blocks, grid, tile_s, fill_s, cell_ref, got_ref, feat_ref, w_hidden, w_pred, out_ref, pair, count_s):
    def clear(i, carry):
        count_s[i] = 0
        return carry

    lax.fori_loop(0, grid[0] * grid[1], clear, 0, unroll=16)

    def one(b, carry):
        owner = peer_of(tile_s[b], grid)
        rank = count_s[owner]
        count_s[owner] = rank + 1
        rows = pl.ds(pl.multiple_of(rank * CH, CH), CH)
        code = jnp.where(lane_index((1, LANES)) < fill_s[b], cell_ref[pl.ds(b, 1), :], -1)
        values = dot(got_ref[owner, rows, :], one_hot(code.astype(F32)))
        pair[:CH, block_lanes(b)] = values.astype(BF)
        return carry

    lax.fori_loop(0, blocks, one, 0, unroll=16)
    pair[CH:, :] = feat_ref[...]
    span = 2048
    for start in range(0, blocks * LANES, span):
        lanes = slice(start, start + span)
        value = gelu_value(dot(w_hidden[...], pair[:, lanes])).astype(BF)
        out_ref[:, lanes] = dot(w_pred[...], value).astype(BF)


def home_predictions(tile, fill, cells, got, features, w_hidden, w_pred, grid):
    devices = grid[0] * grid[1]
    blocks = tile.shape[0]
    return pl.pallas_call(
        functools.partial(home_kernel, blocks, grid),
        in_specs=[smem(), smem()] + [vmem()] * 5,
        out_specs=vmem(),
        out_shape=jax.ShapeDtypeStruct((CH, blocks * LANES), BF),
        scratch_shapes=[
            pltpu.VMEM((2 * CH, blocks * LANES), BF),
            pltpu.SMEM((devices,), jnp.int32),
        ],
        compiler_params=params(),
        cost_estimate=cost(2 * 8192 * 128 * 192, 8 << 20, 8192 * 128),
        name="home_predictions",
    )(tile, fill, cells, got, features, w_hidden, w_pred)


def prepare_kernel(conv_in, conv_mid, conv_out, mlp_grid, mlp_part, mlp_out_t, w_in, w_mid, w_out, f_mid, f_out, w_hidden, w_back):
    for conv, out, flip in ((conv_in, w_in, None), (conv_mid, w_mid, f_mid), (conv_out, w_out, f_out)):
        for dr in range(3):
            for dq in range(3):
                rows = slice(dq * CH, (dq + 1) * CH)
                lanes = slice(dr * CH, (dr + 1) * CH)
                out[rows, lanes] = conv[3 * dr + dq].astype(F32).T.astype(BF)
                if flip is not None:
                    flip[rows, lanes] = conv[8 - 3 * dr - dq]
    w_hidden[:, :CH] = mlp_grid[...].astype(F32).T.astype(BF)
    w_hidden[:, CH:] = mlp_part[...].astype(F32).T.astype(BF)
    w_back[...] = mlp_out_t[...].astype(F32).T.astype(BF)


def prepare(*weights):
    square = jax.ShapeDtypeStruct((3 * CH, 3 * CH), BF)
    shapes = [square] * 5 + [
        jax.ShapeDtypeStruct((HID, 2 * CH), BF),
        jax.ShapeDtypeStruct((HID, CH), BF),
    ]
    return pl.pallas_call(
        prepare_kernel,
        in_specs=[vmem()] * len(weights),
        out_specs=[vmem()] * len(shapes),
        out_shape=shapes,
        compiler_params=params(),
        cost_estimate=cost(0, 1 << 20),
        name="prepare",
    )(*weights)


def swap_blocks(parts):
    parts = list(parts)
    group = lane_index(parts[0].shape) // 16
    for s in (4, 2, 1):
        keep = (group & s) == 0
        for i in range(8):
            if i & s:
                continue
            a, b = parts[i], parts[i + s]
            parts[i] = jnp.where(keep, a, pltpu.roll(b, s * 16, 1))
            parts[i + s] = jnp.where(keep, pltpu.roll(a, LANES - s * 16, 1), b)
    return parts


def patches_to_rows(patch_of, own_ref):
    for part in range(4):
        first, half = part // 2, part % 2
        rows = swap_blocks([patch_of(first * 16 + half * 8 + k) for k in range(8)])
        for r in range(8):
            own_ref[first * 8 + r, :, half * LANES : (half + 1) * LANES] = rows[r].astype(BF)


def write_strips(width, own_ref, head_ref, tail_ref, left_ref, right_ref):
    for r in range(width):
        for half in range(2):
            lanes = slice(half * LANES, (half + 1) * LANES)
            head_ref[2 * r + half] = own_ref[r, :, lanes]
            tail_ref[2 * r + half] = own_ref[CR - width + r, :, lanes]
    group = lane_index((CH, LANES)) // 8
    left = jnp.zeros((CH, LANES), F32)
    right = jnp.zeros((CH, LANES), F32)
    for r in range(CR):
        piece = own_ref[r, :, :LANES].astype(F32)
        left = jnp.where(group == r, pltpu.roll(piece, 8 * r, 1) if r else piece, left)
        piece = own_ref[r, :, LANES:].astype(F32)
        turn = (8 * r + 8) % LANES
        right = jnp.where(group == r, pltpu.roll(piece, turn, 1) if turn else piece, right)
    left_ref[0] = left.astype(BF)
    right_ref[0] = right.astype(BF)


def strip_shapes(width):
    return [
        jax.ShapeDtypeStruct((CR, CH, CC), BF),
        jax.ShapeDtypeStruct((2 * width, CH, LANES), BF),
        jax.ShapeDtypeStruct((2 * width, CH, LANES), BF),
        jax.ShapeDtypeStruct((1, CH, LANES), BF),
        jax.ShapeDtypeStruct((1, CH, LANES), BF),
    ]


def ahead(value, axis):
    count = lax.axis_size(axis)
    return lax.ppermute(value, axis, [(i, i + 1) for i in range(count - 1)])


def behind(value, axis):
    count = lax.axis_size(axis)
    return lax.ppermute(value, axis, [(i + 1, i) for i in range(count - 1)])


def exchange(head, tail, left, right, beside=None):
    from_left, from_right = ahead(right, "gx"), behind(left, "gx")
    above, below = ahead(tail, "gy"), behind(head, "gy")
    if beside is not None:
        from_left, from_right, beside = lax.optimization_barrier((from_left, from_right, beside))
    sides = jnp.concatenate([from_left, from_right], axis=0)
    return (above, below, sides, ahead(sides, "gy"), behind(sides, "gy")), beside


def side_lanes(left, right, r):
    lane = lane_index((CH, LANES))
    turn_right = (LANES - 8 * r) % LANES
    turn_left = (120 - 8 * r) % LANES
    right = pltpu.roll(right, turn_right, 1) if turn_right else right
    left = pltpu.roll(left, turn_left, 1) if turn_left else left
    return jnp.where(lane < 8, right, jnp.where(lane >= 120, left, 0.0)).astype(BF)


def fill_wide(width, wide, own_ref, above_ref, below_ref, sides, above_sides, below_sides):
    left, right = sides[0].astype(F32), sides[1].astype(F32)
    for r in range(CR):
        wide[width + r, :, :CC] = own_ref[r]
        wide[width + r, :, CC:] = side_lanes(left, right, r)
    left, right = above_sides[0].astype(F32), above_sides[1].astype(F32)
    for r in range(width):
        wide[r, :, :LANES] = above_ref[2 * r]
        wide[r, :, LANES:CC] = above_ref[2 * r + 1]
        wide[r, :, CC:] = side_lanes(left, right, CR - width + r)
    left, right = below_sides[0].astype(F32), below_sides[1].astype(F32)
    for r in range(width):
        at = width + CR + r
        wide[at, :, :LANES] = below_ref[2 * r]
        wide[at, :, LANES:CC] = below_ref[2 * r + 1]
        wide[at, :, CC:] = side_lanes(left, right, r)


def conv_row(source, at, weight, shift):
    stacked = source[pl.ds(at, 3)].reshape(3 * CH, WIDE)
    terms = dot(weight, stacked)
    return (
        terms[CH : 2 * CH]
        + pltpu.roll(terms[:CH], shift, 1)
        + pltpu.roll(terms[2 * CH :], WIDE - shift, 1)
    )


def pair_sum(value):
    even = (lane_index(value.shape) & 1) == 0
    return value + jnp.where(even, pltpu.roll(value, WIDE - 1, 1), pltpu.roll(value, 1, 1))


def column_mask(gx, columns):
    lane = lane_index((1, WIDE))
    right = jnp.where(gx < columns - 1, 1.0, 0.0)
    left = jnp.where(gx > 0, 1.0, 0.0)
    return jnp.where(lane < CC, 1.0, jnp.where(lane < CC + 64, right, left))


def one_hot(code):
    cell = lax.broadcasted_iota(jnp.int32, (LANES, LANES), 0).astype(F32).astype(BF)
    code = jnp.broadcast_to(code, (16, LANES)).astype(BF)
    match = cell.reshape(8, 16, LANES) == code[None]
    return jnp.where(match, jnp.ones((), BF), jnp.zeros((), BF)).reshape(LANES, LANES)


def deposit_kernel(per, last, got_ref, own, head, tail, left, right, patch_s, total):
    step = pl.program_id(0)

    @pl.when(step == 0)
    def _():
        total[...] = jnp.zeros_like(total)

    ones = jnp.ones((16, LANES), BF)

    def one(i, carry):
        meta = got_ref[i, 2 * CH :, :].astype(F32)
        for r in range(2):
            feat = jnp.concatenate([got_ref[i, r * CH : (r + 1) * CH, :], ones], axis=0)
            at = meta[2 + r, 0].astype(jnp.int32)
            patch_s[2 * (step * per + i) + r] = at
            total[at] += nt_dot(feat, one_hot(meta[r : r + 1]))
        return carry

    lax.fori_loop(0, per, one, 0, unroll=32)

    @pl.when(step == last)
    def _():
        def patch_of(a):
            value = total[a]
            return value[:CH] / (1.0 + value[CH : CH + 1])

        patches_to_rows(patch_of, own)
        write_strips(HALO_IN, own, head, tail, left, right)


SELF_PATCH = 1


def deposit(got):
    devices = got.shape[0]
    steps = 4
    per = devices // steps
    shapes = strip_shapes(HALO_IN)
    return pl.pallas_call(
        functools.partial(deposit_kernel, per, steps - 1),
        grid=(steps,),
        in_specs=[pl.BlockSpec((per, SLOT_ROWS, LANES), lambda i: (i, 0, 0))],
        out_specs=[whole(s.shape) for s in shapes] + [smem()],
        out_shape=shapes + [jax.ShapeDtypeStruct((2 * devices,), jnp.int32)],
        scratch_shapes=[pltpu.VMEM((NPATCH, CH + 16, LANES), F32)],
        compiler_params=params(),
        cost_estimate=cost(2 * 256 * 80 * 128 * 128, 6 << 20),
        name="deposit",
    )(got)


def forward_kernel(
    columns,
    rows,
    where_s,
    own,
    above,
    below,
    sides,
    above_sides,
    below_sides,
    w_in,
    w_mid,
    w_out,
    patches,
    wide,
    coarse,
    rebuilt,
    slope_in,
    slope_mid,
    fine,
    grid_out,
):
    gx, gy = where_s[0], where_s[1]
    across = column_mask(gx, columns)
    fill_wide(HALO_IN, wide, own, above, below, sides, above_sides, below_sides)

    def row_mask(row):
        at = gy * CR + row
        return jnp.where(jnp.logical_and(at >= 0, at < rows * CR), across, 0.0)

    for g in range(12):
        total = None
        for j in range(2):
            row = 2 * g + j
            pre = conv_row(wide, row, w_in[...], 1)
            value, half, square = gelu_parts(pre)
            if 4 <= row < 4 + CR:
                slope_in[row - 4] = gelu_slope(half[:, :CC], value[:, :CC], square[:, :CC])
                value = jnp.concatenate(
                    [value[:, :CC], value[:, CC:] * across[:, CC:]], axis=1
                ).astype(BF)
            else:
                value = (value * row_mask(row - 4)).astype(BF)
            fine[row] = value
            value = value.astype(F32)
            total = value if j == 0 else total + value
        coarse[g] = (0.25 * pair_sum(total)).astype(BF)

    for g in range(10):
        pre = conv_row(coarse, g, w_mid[...], 2)
        value, slope = gelu_both(pre)
        slope_mid[g] = slope
        before = coarse[g + 1].astype(F32)
        change = (before + value).astype(BF).astype(F32) - before
        for j in range(2):
            row = fine[2 * g + 2 + j].astype(F32) + change
            if 1 <= g < 9:
                rebuilt[2 * g + j, :, :CC] = row[:, :CC].astype(BF)
                rebuilt[2 * g + j, :, CC:] = (row[:, CC:] * across[:, CC:]).astype(BF)
            else:
                rebuilt[2 * g + j] = (row * row_mask(2 * g + j - 2)).astype(BF)

    for r in range(CR):
        grid_out[r] = conv_row(rebuilt, r + 1, w_out[...], 1)[:, :CC]
    for part in range(4):
        first_row, half = part // 2, part % 2
        lanes = slice(half * LANES, (half + 1) * LANES)
        found = swap_blocks([grid_out[first_row * 8 + r, :, lanes] for r in range(8)])
        for k in range(8):
            patches[first_row * 16 + half * 8 + k] = found[k].astype(BF)


def unet_forward(where, halo, w_in, w_mid, w_out, columns, rows):
    shapes = [
        jax.ShapeDtypeStruct((NPATCH, CH, LANES), BF),
        jax.ShapeDtypeStruct((CR + 2 * HALO_IN, CH, WIDE), BF),
        jax.ShapeDtypeStruct((12, CH, WIDE), BF),
        jax.ShapeDtypeStruct((20, CH, WIDE), BF),
        jax.ShapeDtypeStruct((CR, CH, CC), F32),
        jax.ShapeDtypeStruct((10, CH, WIDE), F32),
    ]
    ins = (where, *halo, w_in, w_mid, w_out)
    return pl.pallas_call(
        functools.partial(forward_kernel, columns, rows),
        in_specs=[smem()] + [vmem()] * (len(ins) - 1),
        out_specs=[vmem()] * len(shapes),
        out_shape=shapes,
        scratch_shapes=[pltpu.VMEM((24, CH, WIDE), BF), pltpu.VMEM((CR, CH, CC), F32)],
        compiler_params=params(),
        cost_estimate=cost(2 * 50 * 192 * 192 * 384, 10 << 20, 34 * CH * WIDE),
        name="unet_forward",
    )(*ins)


def share_kernel(per, patch_s, patches, out_ref):
    step = pl.program_id(0)

    def one(i, carry):
        for r in range(2):
            patch = patch_s[2 * (step * per + i) + r]
            out_ref[i, r * CH : (r + 1) * CH, :] = patches[patch]
        return carry

    lax.fori_loop(0, per, one, 0, unroll=16)


def share(patch_at, patches, devices):
    steps = 2
    per = devices // steps
    return pl.pallas_call(
        functools.partial(share_kernel, per),
        grid=(steps,),
        in_specs=[smem(), whole(patches.shape)],
        out_specs=pl.BlockSpec((per, 2 * CH, LANES), lambda i: (i, 0, 0)),
        out_shape=jax.ShapeDtypeStruct((devices, 2 * CH, LANES), BF),
        compiler_params=params(),
        cost_estimate=cost(0, 6 << 20),
        name="share",
    )(patch_at, patches)


GROUP = 16
GROUP_LANES = 2 * GROUP * LANES
PIECES = 1


def particle_kernel(
    last,
    scale,
    patch_s,
    got_ref,
    patches,
    target_ref,
    w_hidden,
    w_pred,
    w_back,
    w_grid,
    own,
    head,
    tail,
    left,
    right,
    grads,
    total,
    pair,
    errors,
):
    step = pl.program_id(0)

    @pl.when(step == 0)
    def _():
        total[...] = jnp.zeros_like(total)
        grads[...] = jnp.zeros_like(grads)

    count = GROUP // PIECES
    span = 2 * count * LANES
    grad_hidden = jnp.zeros((HID, HID), F32)
    grad_pred = jnp.zeros((CH, HID), F32)
    for piece in range(PIECES):
        whole_lanes = slice(piece * span, (piece + 1) * span)
        codes = []
        for k in range(count):
            at = piece * count + k
            meta = got_ref[at, 2 * CH :, :].astype(F32)
            for r in range(2):
                rows = slice(r * CH, (r + 1) * CH)
                start = piece * span + (2 * k + r) * LANES
                lanes = slice(start, start + LANES)
                code = meta[r : r + 1]
                patch = patch_s[2 * (step * GROUP + at) + r]
                pair[:CH, lanes] = dot(patches[patch], one_hot(code)).astype(BF)
                pair[CH:, lanes] = got_ref[at, rows, :]
                codes.append(code)
        inputs = pair[:, whole_lanes]
        hidden, slope = gelu_both(dot(w_hidden[...], inputs))
        hidden = hidden.astype(BF)
        pred = dot(w_pred[...], hidden)
        for k in range(count):
            for r in range(2):
                slot = 2 * k + r
                lanes = slice(slot * LANES, (slot + 1) * LANES)
                live = jnp.where(codes[slot] >= 0.0, scale, 0.0)
                target = target_ref[piece * count + k, r * CH : (r + 1) * CH, :].astype(F32)
                start = piece * span + slot * LANES
                errors[:, start : start + LANES] = (live * (pred[:, lanes] - target)).astype(BF)
        wrong = errors[:, whole_lanes]
        back = (dot(w_back[...], wrong) * slope).astype(BF)
        grad_hidden += nt_dot(inputs, back)
        grad_pred += nt_dot(wrong, hidden)
        given = dot(w_grid[...], back).astype(BF)
        for k in range(count):
            for r in range(2):
                slot = 2 * k + r
                patch = patch_s[2 * (step * GROUP + piece * count + k) + r]
                part = given[:, slot * LANES : (slot + 1) * LANES]
                total[patch] += nt_dot(part, one_hot(codes[slot]))
    grads[:HID] += grad_hidden
    grads[HID:] += grad_pred

    @pl.when(step == last)
    def _():
        patches_to_rows(lambda a: total[a], own)
        write_strips(HALO_OUT, own, head, tail, left, right)


def particles(patch_at, got, patches, target, w_hidden, w_pred, w_back, w_grid, scale):
    devices = got.shape[0]
    steps = devices // GROUP
    shapes = strip_shapes(HALO_OUT) + [jax.ShapeDtypeStruct((HID + CH, HID), F32)]
    return pl.pallas_call(
        functools.partial(particle_kernel, steps - 1, scale),
        grid=(steps,),
        in_specs=[
            smem(),
            pl.BlockSpec((GROUP, SLOT_ROWS, LANES), lambda i: (i, 0, 0)),
            whole(patches.shape),
            pl.BlockSpec((GROUP, 2 * CH, LANES), lambda i: (i, 0, 0)),
            whole(w_hidden.shape),
            whole(w_pred.shape),
            whole(w_back.shape),
            whole(w_grid.shape),
        ],
        out_specs=[whole(s.shape) for s in shapes],
        out_shape=shapes,
        scratch_shapes=[
            pltpu.VMEM((NPATCH, CH, LANES), F32),
            pltpu.VMEM((2 * CH, GROUP_LANES), BF),
            pltpu.VMEM((CH, GROUP_LANES), BF),
        ],
        compiler_params=params(),
        cost_estimate=cost(2 * 32768 * 128 * 700, 16 << 20, 32768 * 128),
        name="particles",
    )(patch_at, got, patches, target, w_hidden, w_pred, w_back, w_grid)


def shifted(value, shift):
    value = jnp.concatenate([value, jnp.zeros((CH, LANES), F32)], axis=1)
    return jnp.concatenate(
        [pltpu.roll(value, WIDE - shift, 1), value, pltpu.roll(value, shift, 1)], axis=0
    ).astype(BF)


def out_terms_kernel(start, own, rebuilt, sum_out):
    sum_out[...] = jnp.zeros_like(sum_out)
    for r in range(start, start + CR // 2):
        sum_out[:, : 3 * CH] += nt_dot(
            rebuilt[r + 1 : r + 4].reshape(3 * CH, WIDE), shifted(own[r].astype(F32), 1)
        )


def out_terms(own, rebuilt, start):
    return pl.pallas_call(
        functools.partial(out_terms_kernel, start),
        in_specs=[vmem(), vmem()],
        out_specs=vmem(),
        out_shape=jax.ShapeDtypeStruct((3 * CH, 2 * LANES), F32),
        compiler_params=params(),
        cost_estimate=cost(2 * 8 * 192 * 192 * 384, 5 << 20),
        name="out_terms",
    )(own, rebuilt)


def backward_kernel(
    columns,
    rows,
    where_s,
    own,
    above,
    below,
    sides,
    above_sides,
    below_sides,
    wide_in,
    coarse,
    slope_in,
    slope_mid,
    flip_mid,
    flip_out,
    particle_grads,
    upper_out,
    lower_out,
    staged,
    wide,
    rebuilt_grad,
    mid_grad,
    first_grad,
    sum_in,
    sum_mid,
):
    gx, gy = where_s[0], where_s[1]
    across = column_mask(gx, columns)
    fill_wide(HALO_OUT, wide, own, above, below, sides, above_sides, below_sides)

    def pooled(g, carry):
        total = None
        for j in range(2):
            value = conv_row(wide, 2 * g + j, flip_out[...], 1).astype(BF)
            rebuilt_grad[2 * g + j] = value
            value = value.astype(F32)
            total = value if j == 0 else total + value
        at = gy * CR + 2 * g - 2
        mask = jnp.where(jnp.logical_and(at >= 0, at < rows * CR), across, 0.0)
        mid_grad[g] = (pair_sum(total) * slope_mid[g] * mask).astype(BF)
        return carry

    for at in range(10):
        pooled(at, 0)

    def fine(g, carry):
        spread = 0.25 * conv_row(mid_grad, g, flip_mid[...], 2)[:, :CC]
        for j in range(2):
            value = rebuilt_grad[2 * g + 2 + j, :, :CC].astype(F32) + spread
            first_grad[2 * g + j] = (value * slope_in[2 * g + j]).astype(BF)
        return carry

    for at in range(8):
        fine(at, 0)

    sum_in[...] = jnp.zeros_like(sum_in)
    sum_mid[...] = jnp.zeros_like(sum_mid)

    def fine_terms(r, carry):
        sum_in[:, : 3 * CH] += nt_dot(
            wide_in[pl.ds(r + HALO_IN - 1, 3)].reshape(3 * CH, WIDE),
            shifted(first_grad[r].astype(F32), 1),
        )
        return carry

    for at in range(CR):
        fine_terms(at, 0)
    even = (lane_index((CH, CC)) & 1) == 0

    def coarse_terms(g, carry):
        value = jnp.where(even, mid_grad[g + 1, :, :CC].astype(F32), 0.0)
        sum_mid[:, : 3 * CH] += nt_dot(
            coarse[pl.ds(g + 1, 3)].reshape(3 * CH, WIDE), shifted(value, 2)
        )
        return carry

    for at in range(8):
        coarse_terms(at, 0)

    rows_each = 3 * CH
    for which, total in enumerate(((sum_in,), (sum_mid,), (upper_out, lower_out))):
        for half in range(2):
            start = (2 * which + half) * rows_each
            lanes = slice(half * LANES, (half + 1) * LANES)
            staged[start : start + rows_each] = sum(part[:, lanes] for part in total).astype(BF)
    start = 6 * rows_each
    staged[start : start + HID + CH] = particle_grads[...].astype(BF)
    staged[start + HID + CH :] = jnp.zeros((REDUCE_ROWS - start - HID - CH, LANES), BF)


def unet_backward(where, halo, saved, flip_mid, flip_out, particle_grads, sums_out, columns, rows):
    ins = (where, *halo, *saved, flip_mid, flip_out, particle_grads, *sums_out)
    return pl.pallas_call(
        functools.partial(backward_kernel, columns, rows),
        in_specs=[smem()] + [vmem()] * (len(ins) - 1),
        out_specs=vmem(),
        out_shape=jax.ShapeDtypeStruct((REDUCE_ROWS, LANES), BF),
        scratch_shapes=[
            pltpu.VMEM((CR + 2 * HALO_OUT, CH, WIDE), BF),
            pltpu.VMEM((20, CH, WIDE), BF),
            pltpu.VMEM((10, CH, WIDE), BF),
            pltpu.VMEM((CR, CH, CC), BF),
            pltpu.VMEM((3 * CH, 2 * LANES), F32),
            pltpu.VMEM((3 * CH, 2 * LANES), F32),
        ],
        compiler_params=params(),
        cost_estimate=cost(2 * 70 * 192 * 192 * 384, 10 << 20),
        name="unet_backward",
    )(*ins)


def split_kernel(sums, grad_in, grad_mid, grad_out, grad_grid, grad_part, grad_pred):
    for which, out in enumerate((grad_in, grad_mid, grad_out)):
        for dr in range(3):
            start = 2 * which * 3 * CH + dr * CH
            low = sums[start : start + CH, :].astype(F32)
            out[3 * dr] = low[:, :CH]
            out[3 * dr + 1] = low[:, CH:]
            out[3 * dr + 2] = sums[start + 3 * CH : start + 4 * CH, :CH].astype(F32)
    start = 18 * CH
    grad_grid[...] = sums[start : start + CH, :].astype(F32)
    grad_part[...] = sums[start + CH : start + 2 * CH, :].astype(F32)
    grad_pred[...] = sums[start + 2 * CH : start + 3 * CH, :].astype(F32)


def split(sums):
    conv = jax.ShapeDtypeStruct((9, CH, CH), F32)
    mlp = jax.ShapeDtypeStruct((CH, HID), F32)
    shapes = [conv, conv, conv, mlp, mlp, mlp]
    return pl.pallas_call(
        split_kernel,
        in_specs=[vmem()],
        out_specs=[vmem()] * 6,
        out_shape=shapes,
        compiler_params=params(),
        cost_estimate=cost(0, 3 << 20),
        name="split",
    )(sums)


def swap(value, axes=("gx", "gy")):
    return lax.all_to_all(value, axes, split_axis=0, concat_axis=0, tiled=True)


def shards(
    part_feat,
    target,
    block_tile,
    block_patch,
    cell_idx,
    block_fill,
    conv_in,
    conv_mid,
    conv_out,
    mlp_grid,
    mlp_part,
    mlp_out,
):
    nblocks = block_tile.shape[0]
    columns, rows = lax.axis_size("gx"), lax.axis_size("gy")
    devices, grid = columns * rows, (columns, rows)
    tile = block_tile[:, 0]
    where = jnp.stack([lax.axis_index("gx"), lax.axis_index("gy")]).astype(jnp.int32)
    scale = 1.0 / math.sqrt(nblocks * LANES * devices)
    w_pred = mlp_out.T
    by_row = ("gy", "gx")

    sent = dispatch(tile, block_patch, block_fill, cell_idx, part_feat, grid)
    sent_target = dispatch_target(tile, target, grid)
    got = swap(sent, by_row)
    prepared = prepare(conv_in, conv_mid, conv_out, mlp_grid, mlp_part, w_pred)
    got, sent_target, where, *prepared = lax.optimization_barrier(
        (got, sent_target, where, *prepared)
    )
    w_in, w_mid, w_out, f_mid, f_out, w_hidden, w_back = prepared
    got_target = swap(sent_target, by_row)

    own, *strips, patch_at = deposit(got)
    strips, _ = exchange(*strips)
    halo = (own, *strips)
    patches, wide_in, coarse, rebuilt, slope_in, slope_mid = unet_forward(
        where, halo, w_in, w_mid, w_out, columns, rows
    )
    got_values = swap(share(patch_at, patches, devices), by_row)
    own, *strips, particle_grads = particles(
        patch_at, got, patches, got_target, w_hidden, w_pred, w_back, mlp_grid, scale
    )
    strips, upper_out = exchange(*strips, out_terms(own, rebuilt, 0))
    sums_out = (upper_out, out_terms(own, rebuilt, CR // 2))
    halo = (own, *strips)
    saved = (wide_in, coarse, slope_in, slope_mid)
    staged = unet_backward(
        where, halo, saved, f_mid, f_out, particle_grads, sums_out, columns, rows
    )
    staged, got_values = lax.optimization_barrier((staged, got_values))
    terms = swap(staged.reshape(devices, REDUCE_ROWS // devices, LANES))
    mine = jnp.sum(terms.astype(F32), axis=0).astype(BF)
    spread = swap(jnp.broadcast_to(mine[None], (devices, *mine.shape)))
    pred = home_predictions(
        tile, block_fill, cell_idx, got_values, part_feat, w_hidden, w_pred, grid
    )
    *grads, grad_pred = split(spread.reshape(REDUCE_ROWS, LANES))
    return (pred, *grads, grad_pred.T)


def solution(mesh):
    return jax.shard_map(
        shards,
        mesh=mesh,
        in_specs=(
            P(None, ("gx", "gy")),
            P(None, ("gx", "gy")),
            P(("gx", "gy"), None),
            P(("gx", "gy")),
            P(("gx", "gy"), None),
            P(("gx", "gy")),
            P(),
            P(),
            P(),
            P(),
            P(),
            P(),
        ),
        out_specs=(P(None, ("gx", "gy")), P(), P(), P(), P(), P(), P()),
        check_vma=False,
    )
```
